512 devices in a mesh: ex: 32 (over y, x, core), fac: 16 (over z).
Axes of the slice: x: 4, y: 4, z: 16, core: 2. Of those that a mesh axis runs over, the one named last changes fastest.
Arguments:
- samples: bfloat16 [32768, 1024], P('ex'), may hold values from -6 to 6
- counts: int32 [32], P('ex'), may hold values from 256 to 1024, as said below
- panel_weight: bfloat16 [1024, 1024], P(None, 'fac'), may hold values from -0.1875 to 0.1875
- rest_weight: bfloat16 [1024, 11264], P(None, 'fac'), may hold values from -0.1875 to 0.1875
Outputs:
- panel_factor: float32 [1024, 1024], P('fac')
- rest_factor: float32 [11264, 1024], P(('fac', 'ex'))
The draws below stay inside these ranges and needn't reach their ends.
Inputs may be any that keep to these rules, and one draw needn't show every extreme that they name: `counts`: live examples of a slab; some slab is full in every draw.
All inputs are finite; a program needn't handle non-finite values.
Results may differ from the reference program's by a relative error of at most 0.018.
Values may be sent and summed in bfloat16 or wider, within the bound.
A program may use at most 64 MiB of HBM per device.

```python
import jax
import jax.numpy as jnp
from jax import lax

DIN = 1024
PANEL = 1024
R_DEV = 1024
REST = 11264
SLABS = 32
EXAMPLES = 32768


def draw_counts(key, part):
    key = jax.random.fold_in(key, 7)
    first, second = jax.random.split(key)
    values = jax.random.randint(first, (SLABS,), R_DEV // 4, R_DEV + 1)
    full_slab = jax.random.randint(second, (), 0, SLABS)
    return jnp.where(jnp.arange(SLABS) == full_slab, R_DEV, values).astype(jnp.int32)


def levels(own_key, extent, cuts, smallest, high):
    gain = 1.0
    for dim, shards_of in cuts:
        draws = jax.random.uniform(jax.random.fold_in(jax.random.fold_in(own_key, 6), dim), (shards_of,), jnp.float32, smallest / len(cuts), high / len(cuts))
        gain = gain * jnp.repeat(jnp.exp(draws), extent[dim] // shards_of).reshape((-1,) + (1,) * (len(extent) - 1 - dim))
    return gain


def scatter_about(key, extent, deviation, limit, pieces=(), kind=jnp.bfloat16):
    drawn = jax.random.normal(key, extent, jnp.float32) * deviation
    if len(pieces) > 0:
        drawn = levels(key, extent, pieces, -0.22, 0.18) * drawn
    return jnp.clip(drawn, min=-limit, max=limit).astype(kind)


def setup_inputs(seed: int = 0) -> dict:
    keys = jax.random.split(jax.random.key(seed), 5)
    return {
        "samples": scatter_about(keys[0], (EXAMPLES, DIN), 1.0, 6.0, ((0, 32),)),
        "counts": draw_counts(jax.random.fold_in(keys[4], 71), 0),
        "panel_weight": scatter_about(keys[2], (DIN, PANEL), DIN ** -0.5, 0.1875, ((1, 16),)),
        "rest_weight": scatter_about(keys[3], (DIN, REST), DIN ** -0.5, 0.1875, ((1, 16),)),
    }


def reference(samples, counts, panel_weight, rest_weight):
    slot = jnp.arange(EXAMPLES, dtype=jnp.int32)
    live = slot % R_DEV < jnp.repeat(counts, R_DEV)
    live = live[:, None]
    panel_feats = jnp.where(live, jax.nn.relu(jnp.dot(samples.astype(jnp.float32), panel_weight.astype(jnp.float32), preferred_element_type=jnp.float32)), 0.0).astype(jnp.bfloat16)
    rest_feats = jnp.where(live, jax.nn.relu(jnp.dot(samples.astype(jnp.float32), rest_weight.astype(jnp.float32), preferred_element_type=jnp.float32)), 0.0).astype(jnp.bfloat16)
    dims = (((0,), (0,)), ((), ()))
    panel_gram = lax.dot_general(panel_feats.astype(jnp.float32), panel_feats.astype(jnp.float32), dims, preferred_element_type=jnp.float32) / EXAMPLES
    panel_gram = panel_gram + jnp.eye(PANEL, dtype=jnp.float32)
    rest_gram = lax.dot_general(rest_feats.astype(jnp.float32), panel_feats.astype(jnp.float32), dims, preferred_element_type=jnp.float32) / EXAMPLES
    panel_factor = jnp.linalg.cholesky(panel_gram)
    rest_factor = lax.linalg.triangular_solve(panel_factor, rest_gram, left_side=False, lower=True, transpose_a=True)
    return (panel_factor, rest_factor)
```

```python
import jax
import jax.numpy as jnp
from jax import lax
from jax.experimental import pallas as pl
from jax.experimental.pallas import tpu as pltpu
from jax.sharding import PartitionSpec as P

F32, BF16 = jnp.float32, jnp.bfloat16
N, B, MB, RR = 1024, 128, 16, 32

def split(x):
    hi = x.astype(BF16)
    return hi, (x - hi.astype(F32)).astype(BF16)

def dot_nt(a, b):
    return lax.dot_general(a, b, (((1,), (1,)), ((), ())), preferred_element_type=F32)

def dot_tn(a, b):
    return lax.dot_general(a, b, (((0,), (0,)), ((), ())), preferred_element_type=F32)

def factor(w):
    sub8 = lax.broadcasted_iota(jnp.int32, (8, B), 0)
    for m in range(B // MB):
        r0 = m * MB
        R = [[w[r0 + 8 * i:r0 + 8 * i + 8, B * h:B * h + B] for h in range(2)] for i in range(MB // 8)]
        C = [[jnp.broadcast_to(R[i][0][:, r0 + t:r0 + t + 1], (8, B)) if 8 * i + 7 >= t else None for i in range(MB // 8)] for t in range(MB)]
        S = [None] * (MB // 8)
        for j in range(MB):
            q, p = divmod(j, 8)
            d = jnp.broadcast_to(C[j][q][p:p + 1, :], (8, B))
            inv = 1.0 / d
            s = lax.rsqrt(d)
            S[q] = s if p == 0 else jnp.where(sub8 >= p, s, S[q])
            rows = [jnp.broadcast_to(R[q][h][p:p + 1, :], (8, B)) for h in range(2)]
            for i in range(q, MB // 8):
                mult = C[j][i] * inv
                if i == q:
                    if p == 7:
                        continue
                    mult = jnp.where(sub8 > p, mult, 0.0)
                for h in range(2):
                    R[i][h] = R[i][h] - mult * rows[h]
                for t in range(j + 1, MB):
                    if C[t][i] is not None:
                        qt, pt = divmod(t, 8)
                        C[t][i] = C[t][i] - mult * jnp.broadcast_to(C[j][qt][pt:pt + 1, :], (8, B))
        U = jnp.concatenate([jnp.concatenate([R[i][0] * S[i], R[i][1] * S[i]], axis=1) for i in range(MB // 8)], axis=0)
        w[r0:r0 + MB, :] = U
        if r0 + MB < B:
            hi, lo = split(U)
            lhs = jnp.concatenate([hi[:, :B], hi[:, :B], lo[:, :B]], axis=0)
            rhs = jnp.concatenate([hi, lo, hi], axis=0)
            upd = dot_tn(lhs, rhs)
            w[r0 + MB:, :] = w[r0 + MB:, :] - upd[r0 + MB:, :]

def factor_kernel(g_ref, rest_ref, l_ref, ro_ref, w, pan, hi_s, lo_s):
    ri = lax.broadcasted_iota(jnp.int32, (B, B), 0)
    ci = lax.broadcasted_iota(jnp.int32, (B, B), 1)
    eye = (ri == ci).astype(F32)
    def step(j, _):
        for c in range(N // B):
            @pl.when(j == c)
            def _():
                r0, K = c * B, c * B
                a = g_ref[r0:, r0:r0 + B]
                b = rest_ref[:, r0:r0 + B]
                a = jnp.concatenate([a, b], axis=0)
                if K:
                    rh, rl = hi_s[r0:r0 + B, :K], lo_s[r0:r0 + B, :K]
                    x = dot_nt(hi_s[r0:, :K], jnp.concatenate([rh, rl], axis=0))
                    a = a - (x[:, :B] + x[:, B:] + dot_nt(lo_s[r0:, :K], rh))
                pan[r0:, :] = a
                w[:, :B] = a[:B, :]
                w[:, B:] = eye
        factor(w)
        for c in range(N // B):
            @pl.when(j == c)
            def _():
                r0 = c * B
                th, tl = split(w[:, B:])
                ah, al = split(pan[r0:, :])
                x = dot_nt(ah, jnp.concatenate([th, tl], axis=0))
                lp = x[:, :B] + x[:, B:] + dot_nt(al, th)
                diag = jnp.where(ri >= ci, lp[:B], 0.0)
                lp = jnp.concatenate([diag, lp[B:]], axis=0)
                h, l = split(lp)
                hi_s[r0:, r0:r0 + B] = h
                lo_s[r0:, r0:r0 + B] = l
                l_ref[r0:, r0:r0 + B] = lp[:N - r0]
                ro_ref[:, r0:r0 + B] = lp[N - r0:]
                if c:
                    l_ref[:r0, r0:r0 + B] = jnp.zeros((r0, B), F32)
        return 0
    lax.fori_loop(0, N // B, step, 0)

def factor_and_solve(g, rest):
    return pl.pallas_call(factor_kernel,
        out_shape=(jax.ShapeDtypeStruct((N, N), F32), jax.ShapeDtypeStruct((RR, N), F32)),
        in_specs=[pl.BlockSpec(memory_space=pltpu.VMEM)] * 2,
        out_specs=(pl.BlockSpec(memory_space=pltpu.VMEM),) * 2,
        scratch_shapes=[pltpu.VMEM((B, 2 * B), F32), pltpu.VMEM((N + RR, B), F32),
                        pltpu.VMEM((N + RR, N), BF16), pltpu.VMEM((N + RR, N), BF16)],
        compiler_params=pltpu.CompilerParams(vmem_limit_bytes=48 * 2**20),
    )(g, rest)


def on_device(samples, counts, panel_weight, rest_weight):
    rows = samples.shape[0]
    total = rows * lax.axis_size("ex")
    live = (jnp.arange(rows, dtype=jnp.int32) < counts[0])[:, None]
    own_width = panel_weight.shape[1]

    def features_of(weight):
        return jnp.where(
            live, jax.nn.relu(jnp.dot(samples, weight, preferred_element_type=F32)), 0.0
        ).astype(BF16)

    own_panel = features_of(panel_weight)
    panel_feats = lax.all_gather(own_panel, "fac", axis=1, tiled=True)
    rest_feats = features_of(rest_weight)
    dims = (((0,), (0,)), ((), ()))
    panel_part = lax.dot_general(own_panel, panel_feats, dims, preferred_element_type=F32)
    share = rest_feats.shape[1] // lax.axis_size("ex")
    rest_part = lax.dot_general(rest_feats, panel_feats, dims, preferred_element_type=F32)
    panel_sum, rest_sum = lax.psum((panel_part, rest_part), "ex")
    rest_rows = lax.dynamic_slice_in_dim(rest_sum, lax.axis_index("ex") * share, share, 0)
    panel_rows = lax.all_gather(panel_sum, "fac", axis=0, tiled=True)
    panel_gram = panel_rows / total + jnp.eye(panel_rows.shape[0], dtype=F32)
    rest_gram = jnp.pad(rest_rows / total, ((0, RR - share), (0, 0)))
    factor, rest_factor = factor_and_solve(panel_gram, rest_gram)
    panel_factor = lax.dynamic_slice_in_dim(factor, lax.axis_index("fac") * own_width, own_width, 0)
    return (panel_factor, rest_factor[:share])


def solution(mesh):
    in_specs = (P("ex", None), P("ex"), P(None, "fac"), P(None, "fac"))
    out_specs = (P("fac", None), P(("fac", "ex"), None))
    return jax.shard_map(
        on_device, mesh=mesh, in_specs=in_specs, out_specs=out_specs, check_vma=False
    )
```

```python
import functools

import jax
import jax.numpy as jnp
from jax import lax
from jax.experimental import pallas as pl
from jax.experimental.pallas import tpu as pltpu
from jax.sharding import PartitionSpec as P

F32, BF16 = jnp.float32, jnp.bfloat16
N, B, MB, RR = 1024, 128, 16, 32
DIN, NE, NZ, NQ = 1024, 32, 16, 16
MESH = pl.DeviceIdType.MESH

def split(x):
    hi = x.astype(BF16)
    return hi, (x - hi.astype(F32)).astype(BF16)

def dot_nt(a, b):
    return lax.dot_general(a, b, (((1,), (1,)), ((), ())), preferred_element_type=F32)

def dot_nn(a, b):
    return jnp.dot(a, b, preferred_element_type=F32)

def dot_tn(a, b):
    return lax.dot_general(a, b, (((0,), (0,)), ((), ())), preferred_element_type=F32)

def factor(w):
    sub8 = lax.broadcasted_iota(jnp.int32, (8, B), 0)
    for m in range(B // MB):
        r0 = m * MB
        R = [[w[r0 + 8 * i:r0 + 8 * i + 8, B * h:B * h + B] for h in range(2)] for i in range(MB // 8)]
        C = [[jnp.broadcast_to(R[i][0][:, r0 + t:r0 + t + 1], (8, B)) if 8 * i + 7 >= t else None for i in range(MB // 8)] for t in range(MB)]
        S = [None] * (MB // 8)
        for j in range(MB):
            q, p = divmod(j, 8)
            d = jnp.broadcast_to(C[j][q][p:p + 1, :], (8, B))
            inv = 1.0 / d
            s = lax.rsqrt(d)
            S[q] = s if p == 0 else jnp.where(sub8 >= p, s, S[q])
            rows = [jnp.broadcast_to(R[q][h][p:p + 1, :], (8, B)) for h in range(2)]
            for i in range(q, MB // 8):
                mult = C[j][i] * inv
                if i == q:
                    if p == 7:
                        continue
                    mult = jnp.where(sub8 > p, mult, 0.0)
                for h in range(2):
                    R[i][h] = R[i][h] - mult * rows[h]
                for t in range(j + 1, MB):
                    if C[t][i] is not None:
                        qt, pt = divmod(t, 8)
                        C[t][i] = C[t][i] - mult * jnp.broadcast_to(C[j][qt][pt:pt + 1, :], (8, B))
        U = jnp.concatenate([jnp.concatenate([R[i][0] * S[i], R[i][1] * S[i]], axis=1) for i in range(MB // 8)], axis=0)
        w[r0:r0 + MB, :] = U
        if r0 + MB < B:
            hi, lo = split(U)
            lhs = jnp.concatenate([hi[:, :B], hi[:, :B], lo[:, :B]], axis=0)
            rhs = jnp.concatenate([hi, lo, hi], axis=0)
            upd = dot_tn(lhs, rhs)
            w[r0 + MB:, :] = w[r0 + MB:, :] - upd[r0 + MB:, :]

def factor_kernel(scale, g_ref, rest_ref, l_ref, ro_ref, w, pan, hi_s, lo_s):
    ri = lax.broadcasted_iota(jnp.int32, (B, B), 0)
    ci = lax.broadcasted_iota(jnp.int32, (B, B), 1)
    eye = (ri == ci).astype(F32)
    def step(j, _):
        for c in range(N // B):
            @pl.when(j == c)
            def _():
                r0, K = c * B, c * B
                a = g_ref[c, r0:, :] * scale
                a = jnp.concatenate([a[:B] + eye] + ([a[B:]] if r0 + B < N else []) + [rest_ref[:, r0:r0 + B] * scale], axis=0)
                if K:
                    rh, rl = hi_s[r0:r0 + B, :K], lo_s[r0:r0 + B, :K]
                    x = dot_nt(hi_s[r0:, :K], jnp.concatenate([rh, rl], axis=0))
                    a = a - (x[:, :B] + x[:, B:] + dot_nt(lo_s[r0:, :K], rh))
                pan[r0:, :] = a
                w[:, :B] = a[:B, :]
                w[:, B:] = eye
        factor(w)
        for c in range(N // B):
            @pl.when(j == c)
            def _():
                r0 = c * B
                th, tl = split(w[:, B:])
                ah, al = split(pan[r0:, :])
                x = dot_nt(ah, jnp.concatenate([th, tl], axis=0))
                lp = x[:, :B] + x[:, B:] + dot_nt(al, th)
                diag = jnp.where(ri >= ci, lp[:B], 0.0)
                lp = jnp.concatenate([diag, lp[B:]], axis=0)
                h, l = split(lp)
                hi_s[r0:, r0:r0 + B] = h
                lo_s[r0:, r0:r0 + B] = l
                l_ref[r0:, r0:r0 + B] = lp[:N - r0]
                ro_ref[:, r0:r0 + B] = lp[N - r0:]
                if c:
                    l_ref[:r0, r0:r0 + B] = jnp.zeros((r0, B), F32)
        return 0
    lax.fori_loop(0, N // B, step, 0)

def factor_and_solve(g, rest, scale):
    return pl.pallas_call(functools.partial(factor_kernel, scale),
        out_shape=(jax.ShapeDtypeStruct((N, N), F32), jax.ShapeDtypeStruct((RR, N), F32)),
        in_specs=[pl.BlockSpec(memory_space=pltpu.VMEM)] * 2,
        out_specs=(pl.BlockSpec(memory_space=pltpu.VMEM),) * 2,
        scratch_shapes=[pltpu.VMEM((B, 2 * B), F32), pltpu.VMEM((N + RR, B), F32),
                        pltpu.VMEM((N + RR, N), BF16), pltpu.VMEM((N + RR, N), BF16)],
        compiler_params=pltpu.CompilerParams(vmem_limit_bytes=48 * 2**20),
    )(g, rest)


SEL = 24


def gram_kernel(shares, x_ref, n_ref, wp_ref, wr_ref, gb, rest_out, xs, wo, wt, pf, wrt, rft, pt, part, prec, zb, rsend, rrecv, sems):
    e, z = lax.axis_index("ex"), lax.axis_index("fac")
    chip, core = e // 2, e % 2
    mate = chip * 2 + 1 - core
    rows = x_ref.shape[0]
    (s_w, r_w, s_p, r_p, s_m, r_m, s_g, r_g, s_z, r_z, s_a, r_a, s_b, r_b, s_r, r_r) = sems

    def z_peer(k):
        return {"fac": (z + k) % NZ}

    def e_peer(k):
        return {"ex": (e + k) % NE}

    def chip_peer(k):
        return {"ex": ((chip + k) % NQ) * 2 + core}

    def each(lo, hi, body):
        def run(k, _):
            body(k)
            return 0
        lax.fori_loop(lo, hi, run, 0)

    barrier = pltpu.get_barrier_semaphore()
    each(1, NZ, lambda k: pl.semaphore_signal(barrier, inc=1, device_id=z_peer(k), device_id_type=MESH))
    each(1, NE, lambda k: pl.semaphore_signal(barrier, inc=1, device_id=e_peer(k), device_id_type=MESH))

    own = wp_ref.shape[1]
    eye = (lax.broadcasted_iota(jnp.int32, (own, own), 0) == lax.broadcasted_iota(jnp.int32, (own, own), 1)).astype(BF16)
    wt_own = dot_nt(eye, wp_ref[...]).astype(BF16)
    wo[...] = wt_own.reshape(4, 16, DIN)
    lanes = pl.ds(pl.multiple_of((e % 8) * 128, 128), 128)
    wt[z, e // 8, :, lanes] = wo[e // 8, :, lanes]
    live = lax.broadcasted_iota(jnp.int32, (rows, 1), 0) < n_ref[0]
    xs[...] = jnp.where(live, x_ref[...].astype(F32), 0.0).astype(BF16)

    def copy(src, dst, send, recv, device):
        return pltpu.make_async_remote_copy(src, dst, send, recv, device_id=device, device_id_type=MESH)

    pl.semaphore_wait(barrier, NZ - 1 + NE - 1)

    def tile(i):
        return wt.at[:, i // 8, :, pl.ds(pl.multiple_of((i % 8) * 128, 128), 128)]

    def z_weight(k, src_z):
        piece = wt.at[src_z, e // 8, :, pl.ds(pl.multiple_of((e % 8) * 128, 128), 128)]
        return copy(piece, piece, s_w.at[k], r_w.at[k], z_peer(k))

    each(1, NZ, lambda k: z_weight(k, z).start())
    span = 256
    wide = wr_ref.shape[1]

    def select(i, _):
        r0 = pl.multiple_of(i * span, span)
        c = lax.broadcasted_iota(jnp.int32, (span, 1), 0).astype(F32) + (i * span).astype(F32)
        b = jnp.floor((c + 0.5) * (1.0 / SEL))
        want = jnp.where(c - SEL * b < shares, c - (SEL - shares) * b, -1.0)
        sel = (lax.broadcasted_iota(jnp.int32, (span, wide), 1).astype(F32) == want).astype(BF16)
        wrt[pl.ds(r0, span), :] = dot_nt(sel, wr_ref[...]).astype(BF16)
        return 0

    lax.fori_loop(0, NE * SEL // span, select, 0)
    each(1, NZ, lambda k: z_weight(k, (z + NZ - k) % NZ).wait_recv())

    def plane_weight(k):
        return copy(tile(e), tile(e), s_p.at[k], r_p.at[k], chip_peer(k))

    def mate_weight(k):
        i = ((chip + NQ - k) % NQ) * 2 + core
        return copy(tile(i), tile(i), s_m.at[k], r_m.at[k], {"ex": mate})

    each(1, NQ, lambda k: plane_weight(k).start())
    mate_weight(0).start()

    def rest_features(i, _):
        r0 = pl.multiple_of(i * span, span)
        f = dot_nt(wrt[pl.ds(r0, span), :], xs[...])
        rft[pl.ds(r0, span), :] = jnp.maximum(f, 0.0).astype(BF16)
        return 0

    lax.fori_loop(0, NE * SEL // span, rest_features, 0)
    pt[...] = jnp.maximum(dot_nt(wt_own, xs[...]), 0.0).astype(BF16)

    def pass_on(k):
        plane_weight(k).wait_recv()
        mate_weight(k).start()

    each(1, NQ, pass_on)
    each(0, NQ, lambda k: mate_weight(k).wait_recv())

    def panel_features(i, _):
        r0 = pl.multiple_of(i * span, span)
        f = dot_nt(xs[pl.ds(r0, span), :], wt[...].reshape(N, DIN))
        pf[pl.ds(r0, span), :] = jnp.maximum(f, 0.0).astype(BF16)
        return 0

    lax.fori_loop(0, rows // span, panel_features, 0)

    mine = dot_nn(pt[...], pf[...])
    for q in range(4):
        for h, lt in ((0, q), (1, 7 - q)):
            part[q * 8:q * 8 + 8, h] = mine[:, lt * 128:lt * 128 + 128].reshape(8, 8, 128)

    def gram_part(k):
        return copy(part.at[(e + k) % NE], prec.at[k], s_g.at[k], r_g.at[k], e_peer(k))

    each(1, NE, lambda k: gram_part(k).start())

    def rest_gram(i, _):
        r0 = pl.multiple_of(i * span, span)
        rsend[pl.ds(r0, span), :] = dot_nn(rft[pl.ds(r0, span), :], pf[...])
        return 0

    lax.fori_loop(0, NE * SEL // span, rest_gram, 0)
    each(1, NE, lambda k: gram_part(k).wait_recv())
    total = lax.fori_loop(1, NE, lambda k, t: t + prec[k], part[e])
    zb[:, z] = total

    def z_gram(k, src_z):
        return copy(zb.at[:, src_z], zb.at[:, src_z], s_z.at[k], r_z.at[k], z_peer(k))

    each(1, NZ, lambda k: z_gram(k, z).start())
    each(1, NZ, lambda k: z_gram(k, (z + NZ - k) % NZ).wait_recv())
    q, rg = e // 8, e % 8
    gb[q, :, rg] = zb[0]
    gb[7 - q, 8:, rg] = zb[1, 8:]

    def left(i):
        return gb.at[i // 8, :, i % 8]

    def right(i):
        return gb.at[7 - i // 8, pl.ds(8, 8), i % 8]

    halves = (left, right)

    def plane_gram(h, k):
        piece = halves[h](e)
        return copy(piece, piece, s_a.at[h * NQ + k], r_a.at[h * NQ + k], chip_peer(k))

    def mate_gram(h, k):
        piece = halves[h](((chip + NQ - k) % NQ) * 2 + core)
        return copy(piece, piece, s_b.at[h * NQ + k], r_b.at[h * NQ + k], {"ex": mate})

    for h in range(2):
        each(1, NQ, lambda k: plane_gram(h, k).start())
        mate_gram(h, 0).start()

    def rest_part(k):
        src = rsend.at[pl.ds(pl.multiple_of(((e + k) % NE) * SEL, 8), SEL), :]
        return copy(src, rrecv.at[k], s_r.at[k], r_r.at[k], e_peer(k))

    each(1, NE, lambda k: rest_part(k).start())

    for h in range(2):
        def pass_gram(k):
            plane_gram(h, k).wait_recv()
            mate_gram(h, k).start()

        each(1, NQ, pass_gram)
    for h in range(2):
        each(0, NQ, lambda k: mate_gram(h, k).wait_recv())
    each(1, NE, lambda k: rest_part(k).wait_recv())
    first = rsend[pl.ds(pl.multiple_of(e * SEL, 8), SEL), :]
    rest_out[:SEL, :] = lax.fori_loop(1, NE, lambda k, t: t + rrecv[k], first)
    rest_out[SEL:, :] = jnp.zeros((RR - SEL, N), F32)

    each(1, NZ, lambda k: z_weight(k, z).wait_send())
    each(1, NQ, lambda k: plane_weight(k).wait_send())
    each(0, NQ, lambda k: mate_weight(k).wait_send())
    each(1, NE, lambda k: gram_part(k).wait_send())
    each(1, NZ, lambda k: z_gram(k, z).wait_send())

    for h in range(2):
        each(1, NQ, lambda k: plane_gram(h, k).wait_send())
        each(0, NQ, lambda k: mate_gram(h, k).wait_send())
    each(1, NE, lambda k: rest_part(k).wait_send())


def gram(samples, counts, panel_weight, rest_weight):
    rows = samples.shape[0]
    own, wide = panel_weight.shape[1], rest_weight.shape[1]
    vmem = pl.BlockSpec(memory_space=pltpu.VMEM)
    counted = [NZ, NZ, NQ, NQ, NQ, NQ, NE, NE, NZ, NZ, 2 * NQ, 2 * NQ, 2 * NQ, 2 * NQ, NE, NE]
    return pl.pallas_call(
        functools.partial(gram_kernel, wide // NE),
        out_shape=(jax.ShapeDtypeStruct((8, NZ, 8, 8, 128), F32), jax.ShapeDtypeStruct((RR, N), F32)),
        in_specs=[vmem, pl.BlockSpec(memory_space=pltpu.SMEM), vmem, vmem],
        out_specs=(vmem, vmem),
        scratch_shapes=[
            pltpu.VMEM((rows, DIN), BF16),
            pltpu.VMEM((4, 16, DIN), BF16),
            pltpu.VMEM((NZ, 4, 16, DIN), BF16),
            pltpu.VMEM((rows, N), BF16),
            pltpu.VMEM((NE * SEL, DIN), BF16),
            pltpu.VMEM((NE * SEL, rows), BF16),
            pltpu.VMEM((own, rows), BF16),
            pltpu.VMEM((NE, 2, 8, 128), F32),
            pltpu.VMEM((NE, 2, 8, 128), F32),
            pltpu.VMEM((2, NZ, 8, 128), F32),
            pltpu.VMEM((NE * SEL, N), F32),
            pltpu.VMEM((NE, SEL, N), F32),
            [pltpu.SemaphoreType.DMA((c,)) for c in counted],
        ],
        compiler_params=pltpu.CompilerParams(
            collective_id=0, has_side_effects=True, vmem_limit_bytes=48 * 2**20
        ),
        cost_estimate=pl.CostEstimate(flops=8 * 2**30, bytes_accessed=8 * 2**20, transcendentals=0),
    )(samples, counts, panel_weight, rest_weight)


def on_device(samples, counts, panel_weight, rest_weight):
    total = samples.shape[0] * NE
    share, own_width = rest_weight.shape[1] // NE, panel_weight.shape[1]
    panel_gram, rest_gram = gram(samples, counts, panel_weight, rest_weight)
    factor, rest_factor = factor_and_solve(panel_gram.reshape(8, N, 128), rest_gram, 1.0 / total)
    panel_factor = lax.dynamic_slice_in_dim(factor, lax.axis_index("fac") * own_width, own_width, 0)
    return (panel_factor, rest_factor[:share])


def solution(mesh):
    in_specs = (P("ex", None), P("ex"), P(None, "fac"), P(None, "fac"))
    out_specs = (P("fac", None), P(("fac", "ex"), None))
    return jax.shard_map(
        on_device, mesh=mesh, in_specs=in_specs, out_specs=out_specs, check_vma=False
    )
```

```python
import functools

import jax
import jax.numpy as jnp
from jax import lax
from jax.experimental import pallas as pl
from jax.experimental.pallas import tpu as pltpu
from jax.sharding import PartitionSpec as P

F32, BF16 = jnp.float32, jnp.bfloat16
MESH = pl.DeviceIdType.MESH
N, DIN, B, MB = 1024, 1024, 128, 16
NE, NZ, NQ = 32, 16, 16
SEL = 24
HALF = NQ * SEL


def split(x):
    hi = x.astype(BF16)
    return hi, (x - hi.astype(F32)).astype(BF16)


def dot_nt(a, b):
    return lax.dot_general(a, b, (((1,), (1,)), ((), ())), preferred_element_type=F32)


def dot_nn(a, b):
    return jnp.dot(a, b, preferred_element_type=F32)


def dot_tn(a, b):
    return lax.dot_general(a, b, (((0,), (0,)), ((), ())), preferred_element_type=F32)


def factor(w):
    row = lax.broadcasted_iota(jnp.int32, (MB, B), 0)
    for m in range(B // MB):
        r0 = m * MB
        R = w[r0:r0 + MB, :]
        C = jnp.stack([jnp.broadcast_to(R[:, r0 + t:r0 + t + 1], (MB, B)) for t in range(MB)], axis=0)
        S = jnp.ones((MB, B), F32)
        for j in range(MB):
            c = C[0]
            d = jnp.broadcast_to(c[j:j + 1, :], (MB, B))
            S = jnp.where(row >= j, lax.rsqrt(d), S)
            if j < MB - 1:
                mult = jnp.where(row > j, c * (1.0 / d), 0.0)
                R = R - jnp.concatenate([mult, mult], axis=1) * R[j:j + 1, :]
                C = C[1:] - mult[None] * C[1:, j:j + 1, :]
        U = R * jnp.concatenate([S, S], axis=1)
        w[r0:r0 + MB, :] = U
        if r0 + MB < B:
            hi, lo = split(U)
            lhs = jnp.concatenate([hi[:, :B], hi[:, :B], lo[:, :B]], axis=0)
            rhs = jnp.concatenate([hi, lo, hi], axis=0)
            upd = dot_tn(lhs, rhs)
            w[r0 + MB:, :] = w[r0 + MB:, :] - upd[r0 + MB:, :]


def times_split(hi, lo, b2):
    x = dot_nt(hi, b2)
    return x[:, :B] + x[:, B:] + dot_nt(lo, b2[:B])


def kernel(share, scale, x_ref, n_ref, wp_ref, wr_ref, panel_out, rest_out,
           xs, wr, wt, pf, wrt, rft, pt, part, prec, zb, gb, rsend, rmate, rrecv, w, pan, hi_s, lo_s, tts, xh, xl, loc, sems):
    e, z = lax.axis_index("ex"), lax.axis_index("fac")
    chip, core = e // 2, e % 2
    mate = {"ex": chip * 2 + 1 - core}
    lq, rg, zg = e // 8, e % 8, z // 4
    rows, own, wide = xs.shape[0], wp_ref.shape[0], wr_ref.shape[0]
    (s_w, r_w, s_p, r_p, s_m, r_m, s_g, r_g, s_z, r_z, s_a, r_a, s_b, r_b, s_r, r_r, s_h, r_h) = sems

    def z_peer(k):
        return {"fac": (z + k) % NZ}

    def e_peer(k):
        return {"ex": (e + k) % NE}

    def chip_peer(k):
        return {"ex": ((chip + k) % NQ) * 2 + core}

    def chip_from(k):
        return ((chip + NQ - k) % NQ) * 2 + core

    def each(lo, hi, body):
        def run(k, _):
            body(k)
            return 0
        lax.fori_loop(lo, hi, run, 0)

    def blocks(count, span, body):
        each(0, count, lambda i: body(pl.ds(pl.multiple_of(i * span, span), span)))

    def copy(src, dst, send, recv, device):
        return pltpu.make_async_remote_copy(src, dst, send, recv, device_id=device, device_id_type=MESH)

    def lanes(i):
        return pl.ds(pl.multiple_of((i % 8) * 128, 128), 128)

    barrier = pltpu.get_barrier_semaphore()
    each(1, NZ, lambda k: pl.semaphore_signal(barrier, inc=1, device_id=z_peer(k), device_id_type=MESH))
    each(1, NE, lambda k: pl.semaphore_signal(barrier, inc=1, device_id=e_peer(k), device_id_type=MESH))
    own_tile = wp_ref.at[pl.ds(pl.multiple_of((e // 8) * 16, 16), 16), lanes(e)]
    local = [
        pltpu.make_async_copy(own_tile, wt.at[z, e // 8, :, lanes(e)], loc.at[0]),
        pltpu.make_async_copy(x_ref, xs, loc.at[1]),
        pltpu.make_async_copy(wr_ref, wr, loc.at[2]),
        pltpu.make_async_copy(wp_ref, pt, loc.at[3]),
    ]
    for c in local:
        c.start()
    pl.semaphore_wait(barrier, NZ - 1 + NE - 1)

    def tile(i):
        return wt.at[:, i // 8, :, lanes(i)]

    def z_weight(k, src_z):
        return copy(own_tile, wt.at[src_z, e // 8, :, lanes(e)], s_w.at[k], r_w.at[k], z_peer(k))

    each(1, NZ, lambda k: z_weight(k, z).start())
    for c in local:
        c.wait()

    def mask(at):
        live = lax.broadcasted_iota(jnp.int32, (256, 1), 0) + at.start < n_ref[0]
        xs[at, :] = jnp.where(live, xs[at, :].astype(F32), 0.0).astype(BF16)

    blocks(rows // 256, 256, mask)

    def select(at):
        c = (lax.broadcasted_iota(jnp.int32, (128, 1), 0) + at.start).astype(F32)
        b = jnp.floor((c + 0.5) * (1.0 / SEL))
        t = c - SEL * b
        device = jnp.where(b < NQ, 2 * b, 2 * (b - NQ) + 1)
        want = jnp.where(t < share, device * share + t, -1.0)
        sel = (lax.broadcasted_iota(jnp.int32, (128, wide), 1).astype(F32) == want).astype(BF16)
        wrt[at, :] = dot_nn(sel, wr[...]).astype(BF16)

    blocks(NE * SEL // 128, 128, select)
    each(1, NZ, lambda k: z_weight(k, (z + NZ - k) % NZ).wait_recv())

    def plane_weight(k):
        return copy(tile(e), tile(e), s_p.at[k], r_p.at[k], chip_peer(k))

    def mate_weight(k):
        i = chip_from(k)
        return copy(tile(i), tile(i), s_m.at[k], r_m.at[k], mate)

    each(1, NQ, lambda k: plane_weight(k).start())
    mate_weight(0).start()

    def rest_features(at):
        rft[at, :] = jnp.maximum(dot_nt(wrt[at, :], xs[...]), 0.0).astype(BF16)

    blocks(NE * SEL // 256, 256, rest_features)
    pt[...] = jnp.maximum(dot_nt(pt[...], xs[...]), 0.0).astype(BF16)

    def pass_on(k):
        plane_weight(k).wait_recv()
        mate_weight(k).start()

    each(1, NQ, pass_on)
    each(0, NQ, lambda k: mate_weight(k).wait_recv())

    def panel_features(at):
        pf[at, :] = jnp.maximum(dot_nt(xs[at, :], wt[...].reshape(N, DIN)), 0.0).astype(BF16)

    blocks(rows // 256, 256, panel_features)

    mine = dot_nn(pt[...], pf[...])
    for lt in range(8):
        part[lt // 4, lt % 4] = mine[:, lt * 128:lt * 128 + 128].reshape(8, 8, 128)

    def gram_part(k):
        i = (e + k) % NE
        return copy(part.at[:, (i // 8 + 4 - zg) % 4, i % 8], prec.at[k], s_g.at[k], r_g.at[k], e_peer(k))

    each(1, NE, lambda k: gram_part(k).start())

    def rest_gram(c):
        at = pl.ds(pl.multiple_of(c * HALF, HALF), HALF)
        rsend[c] = dot_nn(rft[at, :], pf[...]).reshape(NQ, SEL, N)

    rest_half = copy(rsend.at[1 - core], rmate, s_h.at[0], r_h.at[0], mate)
    rest_gram(1 - core)
    rest_half.start()
    each(1, NE, lambda k: gram_part(k).wait_recv())
    zb[:, z] = lax.fori_loop(1, NE, lambda k, t: t + prec[k], part[:, (lq + 4 - zg) % 4, rg])

    def z_gram(k, src_z):
        return copy(zb.at[:, src_z], zb.at[:, src_z], s_z.at[k], r_z.at[k], z_peer(k))

    each(1, NZ, lambda k: z_gram(k, z).start())
    rest_gram(core)
    each(1, NZ, lambda k: z_gram(k, (z + NZ - k) % NZ).wait_recv())

    def group(i, lt):
        return (i // 8 + 8 - lt) % 4

    def needed(i, lt, run):
        pl.when(group(i, lt) >= lt // 2)(run)

    def panel_piece(i, lt):
        return gb.at[lt, pl.ds(group(i, lt) * 4, 4), i % 8]

    def plane_gram(lt, k):
        src = zb.at[lt // 4, pl.ds(group(e, lt) * 4, 4)]
        return copy(src, panel_piece(e, lt), s_a.at[lt * NQ + k], r_a.at[lt * NQ + k], chip_peer(k))

    def from_plane(lt, k):
        piece = panel_piece(chip_from(k), lt)
        return copy(piece, piece, s_a.at[lt * NQ + k], r_a.at[lt * NQ + k], chip_peer(k))

    def mate_gram(lt, k):
        piece = panel_piece(chip_from(k), lt)
        return copy(piece, piece, s_b.at[lt * NQ + k], r_b.at[lt * NQ + k], mate)

    def from_mate(lt, k):
        piece = panel_piece(((chip + NQ - k) % NQ) * 2 + 1 - core, lt)
        return copy(piece, piece, s_b.at[lt * NQ + k], r_b.at[lt * NQ + k], mate)

    def send_panel(lt):
        def run():
            gb[lt, pl.ds(group(e, lt) * 4, 4), rg] = zb[lt // 4, pl.ds(group(e, lt) * 4, 4)]
            each(1, NQ, lambda k: plane_gram(lt, k).start())
            mate_gram(lt, 0).start()
        needed(e, lt, run)

    each(0, N // B, send_panel)

    rest_half.wait_recv()

    def add_mate(i):
        rsend[core, i] = rsend[core, i] + rmate[i]

    each(0, NQ, add_mate)

    def rest_part(k):
        return copy(rsend.at[core, (chip + k) % NQ], rrecv.at[k], s_r.at[k], r_r.at[k], chip_peer(k))

    each(1, NQ, lambda k: rest_part(k).start())

    def pass_panel(lt):
        def run(k):
            def go():
                from_plane(lt, k).wait_recv()
                mate_gram(lt, k).start()
            needed(chip_from(k), lt, go)
        each(1, NQ, run)

    def wait_panel(lt):
        def run(k):
            needed(((chip + NQ - k) % NQ) * 2 + 1 - core, lt, lambda: from_mate(lt, k).wait_recv())
        each(0, NQ, run)

    ri = lax.broadcasted_iota(jnp.int32, (B, B), 0)
    ci = lax.broadcasted_iota(jnp.int32, (B, B), 1)
    eye = (ri == ci).astype(F32)
    pass_panel(0)

    def step(j):
        wait_panel(j)
        for c in range(N // B):
            @pl.when(j == c)
            def _():
                r0 = c * B
                a = gb[c, 2 * c:].reshape(N - r0, B) * scale
                a = jnp.concatenate([a[:B] + eye] + ([a[B:]] if r0 + B < N else []), axis=0)
                if c:
                    b2 = jnp.concatenate([hi_s[r0:r0 + B, :r0], lo_s[r0:r0 + B, :r0]], axis=0)
                    a = a - times_split(hi_s[r0:, :r0], lo_s[r0:, :r0], b2)
                pan[r0:, :] = a
                w[:, :B] = a[:B, :]
                w[:, B:] = eye

        pl.when(j < N // B - 1)(lambda: pass_panel(j + 1))
        factor(w)
        for c in range(N // B):
            @pl.when(j == c)
            def _():
                r0 = c * B
                t2 = jnp.concatenate(split(w[:, B:]), axis=0)
                tts[c] = t2
                ah, al = split(pan[r0:, :])
                lp = times_split(ah, al, t2)
                lp = jnp.concatenate([jnp.where(ri >= ci, lp[:B], 0.0)] + ([lp[B:]] if r0 + B < N else []), axis=0)
                h, l = split(lp)
                hi_s[r0:, r0:r0 + B] = h
                lo_s[r0:, r0:r0 + B] = l
                pan[r0:, :] = lp
                ours = pan[pl.ds(pl.multiple_of(z * own, own), own), :]
                panel_out[:, r0:r0 + B] = jnp.where(z >= 2 * c, ours, 0.0)

    each(0, N // B, step)

    each(1, NQ, lambda k: rest_part(k).wait_recv())
    total = lax.fori_loop(1, NQ, lambda k, t: t + rrecv[k], rsend[core, chip]) * scale
    for c in range(N // B):
        r0 = c * B
        a = total[:, r0:r0 + B]
        if c:
            b2 = jnp.concatenate([hi_s[r0:r0 + B, :r0], lo_s[r0:r0 + B, :r0]], axis=0)
            a = a - times_split(xh[:SEL, :r0], xl[:SEL, :r0], b2)
        ah, al = split(a)
        a = times_split(ah, al, tts[c])
        rest_out[:, r0:r0 + B] = a[:share]
        h, l = split(a)
        xh[:SEL, r0:r0 + B] = h
        xl[:SEL, r0:r0 + B] = l

    each(1, NZ, lambda k: z_weight(k, z).wait_send())
    each(1, NQ, lambda k: plane_weight(k).wait_send())
    each(0, NQ, lambda k: mate_weight(k).wait_send())
    each(1, NE, lambda k: gram_part(k).wait_send())
    each(1, NZ, lambda k: z_gram(k, z).wait_send())
    rest_half.wait_send()
    each(1, NQ, lambda k: rest_part(k).wait_send())

    def panel_sent(lt):
        needed(e, lt, lambda: each(1, NQ, lambda k: plane_gram(lt, k).wait_send()))
        each(0, NQ, lambda k: needed(chip_from(k), lt, lambda: mate_gram(lt, k).wait_send()))

    each(0, N // B, panel_sent)


def on_device(samples, counts, panel_weight, rest_weight):
    rows = samples.shape[0]
    own, wide = panel_weight.shape[1], rest_weight.shape[1]
    share = wide // NE
    vmem, anywhere = pl.BlockSpec(memory_space=pltpu.VMEM), pl.BlockSpec(memory_space=pl.ANY)
    counted = [NZ, NZ, NQ, NQ, NQ, NQ, NE, NE, NZ, NZ, 8 * NQ, 8 * NQ, 8 * NQ, 8 * NQ, NQ, NQ, 1, 1]
    return pl.pallas_call(
        functools.partial(kernel, share, 1.0 / (rows * NE)),
        out_shape=(jax.ShapeDtypeStruct((own, N), F32), jax.ShapeDtypeStruct((share, N), F32)),
        in_specs=[anywhere, pl.BlockSpec(memory_space=pltpu.SMEM), anywhere, anywhere],
        out_specs=(vmem, vmem),
        scratch_shapes=[
            pltpu.VMEM((rows, DIN), BF16),
            pltpu.VMEM((wide, DIN), BF16),
            pltpu.VMEM((NZ, 4, 16, DIN), BF16),
            pltpu.VMEM((rows, N), BF16),
            pltpu.VMEM((NE * SEL, DIN), BF16),
            pltpu.VMEM((NE * SEL, rows), BF16),
            pltpu.VMEM((own, rows), BF16),
            pltpu.VMEM((2, 4, 8, 8, 128), F32),
            pltpu.VMEM((NE, 2, 8, 128), F32),
            pltpu.VMEM((2, NZ, 8, 128), F32),
            pltpu.VMEM((8, NZ, 8, 8, 128), F32),
            pltpu.VMEM((2, NQ, SEL, N), F32),
            pltpu.VMEM((NQ, SEL, N), F32),
            pltpu.VMEM((NQ, SEL, N), F32),
            pltpu.VMEM((B, 2 * B), F32),
            pltpu.VMEM((N, B), F32),
            pltpu.VMEM((N, N), BF16),
            pltpu.VMEM((N, N), BF16),
            pltpu.VMEM((8, 2 * B, B), BF16),
            pltpu.VMEM((32, N), BF16),
            pltpu.VMEM((32, N), BF16),
            pltpu.SemaphoreType.DMA((4,)),
            [pltpu.SemaphoreType.DMA((c,)) for c in counted],
        ],
        compiler_params=pltpu.CompilerParams(
            collective_id=0, has_side_effects=True, vmem_limit_bytes=52 * 2**20
        ),
        cost_estimate=pl.CostEstimate(flops=10 * 2**30, bytes_accessed=8 * 2**20, transcendentals=0),
    )(samples, counts, panel_weight.T, rest_weight.T)


def solution(mesh):
    in_specs = (P("ex", None), P("ex"), P(None, "fac"), P(None, "fac"))
    out_specs = (P("fac", None), P(("fac", "ex"), None))
    return jax.shard_map(
        on_device, mesh=mesh, in_specs=in_specs, out_specs=out_specs, check_vma=False
    )
```

```python
import functools

import jax
import jax.numpy as jnp
from jax import lax
from jax.experimental import pallas as pl
from jax.experimental.pallas import tpu as pltpu
from jax.sharding import PartitionSpec as P

F32, BF16 = jnp.float32, jnp.bfloat16
MESH = pl.DeviceIdType.MESH
N, DIN, B, MB = 1024, 1024, 128, 16
NE, NZ, NQ = 32, 16, 16
SEL = 24
HALF = NQ * SEL


def split(x):
    hi = x.astype(BF16)
    return hi, (x - hi.astype(F32)).astype(BF16)


def dot_nt(a, b):
    return lax.dot_general(a, b, (((1,), (1,)), ((), ())), preferred_element_type=F32)


def dot_nn(a, b):
    return jnp.dot(a, b, preferred_element_type=F32)


def dot_tn(a, b):
    return lax.dot_general(a, b, (((0,), (0,)), ((), ())), preferred_element_type=F32)


def factor(w):
    row = lax.broadcasted_iota(jnp.int32, (MB, B), 0)
    for m in range(B // MB):
        r0 = m * MB
        R = w[r0:r0 + MB, :]
        C = jnp.stack([jnp.broadcast_to(R[:, r0 + t:r0 + t + 1], (MB, B)) for t in range(MB)], axis=0)
        S = jnp.ones((MB, B), F32)
        for j in range(MB):
            c = C[0]
            d = jnp.broadcast_to(c[j:j + 1, :], (MB, B))
            S = jnp.where(row >= j, lax.rsqrt(d), S)
            if j < MB - 1:
                mult = jnp.where(row > j, c * (1.0 / d), 0.0)
                R = R - jnp.concatenate([mult, mult], axis=1) * R[j:j + 1, :]
                C = C[1:] - mult[None] * C[1:, j:j + 1, :]
        U = R * jnp.concatenate([S, S], axis=1)
        w[r0:r0 + MB, :] = U
        if r0 + MB < B:
            hi, lo = split(U)
            lhs = jnp.concatenate([hi[:, :B], hi[:, :B], lo[:, :B]], axis=0)
            rhs = jnp.concatenate([hi, lo, hi], axis=0)
            upd = dot_tn(lhs, rhs)
            w[r0 + MB:, :] = w[r0 + MB:, :] - upd[r0 + MB:, :]


def times_split(hi, lo, b2):
    x = dot_nt(hi, b2)
    return x[:, :B] + x[:, B:] + dot_nt(lo, b2[:B])


def kernel(share, scale, x_ref, n_ref, wp_ref, wr_ref, panel_out, rest_out,
           xs, wr, wt, pf, wrt, rft, pt, part, prec, zb, gb, rsend, rmate, rrecv, w, pan, hi_s, lo_s, tts, xh, xl, loc, sems):
    e, z = lax.axis_index("ex"), lax.axis_index("fac")
    chip, core = e // 2, e % 2
    mate = {"ex": chip * 2 + 1 - core}
    lq, rg, zg = chip // 4, core * 4 + chip % 4, z // 4
    rows, own, wide = xs.shape[0], wp_ref.shape[0], wr_ref.shape[0]
    (s_w, r_w, s_p, r_p, s_m, r_m, s_g, r_g, s_z, r_z, s_a, r_a, s_b, r_b, s_r, r_r, s_h, r_h) = sems

    def z_peer(k):
        return {"fac": (z + k) % NZ}

    def e_peer(k):
        return {"ex": (e + k) % NE}

    def chip_peer(k):
        return {"ex": ((chip + k) % NQ) * 2 + core}

    def each(lo, hi, body):
        def run(k, _):
            body(k)
            return 0
        lax.fori_loop(lo, hi, run, 0)

    def unrolled(lo, hi, body):
        for k in range(lo, hi):
            body(k)

    def blocks(count, span, body):
        each(0, count, lambda i: body(pl.ds(pl.multiple_of(i * span, span), span)))

    def copy(src, dst, send, recv, device):
        return pltpu.make_async_remote_copy(src, dst, send, recv, device_id=device, device_id_type=MESH)

    def arrived(ref, sem):
        pltpu.make_async_copy(ref, ref, sem).wait()

    def lanes(i, count=1):
        return pl.ds(pl.multiple_of(i * 128, 128), 128 * count)

    barrier = pltpu.get_barrier_semaphore()
    unrolled(1, NZ, lambda k: pl.semaphore_signal(barrier, inc=1, device_id=z_peer(k), device_id_type=MESH))
    unrolled(1, NE, lambda k: pl.semaphore_signal(barrier, inc=1, device_id=e_peer(k), device_id_type=MESH))
    own_tile = wp_ref.at[pl.ds(pl.multiple_of(lq * 16, 16), 16), lanes(rg)]
    local = [
        pltpu.make_async_copy(own_tile, wt.at[z, lq, :, lanes(rg)], loc.at[0]),
        pltpu.make_async_copy(x_ref, xs, loc.at[1]),
        pltpu.make_async_copy(wr_ref, wr, loc.at[2]),
        pltpu.make_async_copy(wp_ref, pt, loc.at[3]),
    ]
    for c in local:
        c.start()
    pl.semaphore_wait(barrier, NZ - 1 + NE - 1)

    def z_weight(k):
        return copy(own_tile, wt.at[z, lq, :, lanes(rg)], s_w.at[0], r_w.at[0], z_peer(k))

    unrolled(1, NZ, lambda k: z_weight(k).start())
    local[0].wait()
    arrived(wt.at[pl.ds(0, NZ - 1), lq, :, lanes(rg)], r_w.at[0])

    tile = wt.at[:, lq, :, lanes(rg)]
    unrolled(1, NQ, lambda k: copy(tile, tile, s_p.at[0], r_p.at[lq], chip_peer(k)).start())

    def pass_weight(y):
        piece = wt.at[:, y, :, lanes(core * 4, 4)]
        copy(piece, piece, s_m.at[y], r_m.at[y], mate).start()

    for c in local[1:]:
        c.wait()

    def mask(at):
        live = lax.broadcasted_iota(jnp.int32, (256, 1), 0) + at.start < n_ref[0]
        xs[at, :] = jnp.where(live, xs[at, :].astype(F32), 0.0).astype(BF16)

    blocks(rows // 256, 256, mask)

    def select(at):
        c = (lax.broadcasted_iota(jnp.int32, (128, 1), 0) + at.start).astype(F32)
        b = jnp.floor((c + 0.5) * (1.0 / SEL))
        t = c - SEL * b
        device = jnp.where(b < NQ, 2 * b, 2 * (b - NQ) + 1)
        want = jnp.where(t < share, device * share + t, -1.0)
        sel = (lax.broadcasted_iota(jnp.int32, (128, wide), 1).astype(F32) == want).astype(BF16)
        wrt[at, :] = dot_nn(sel, wr[...]).astype(BF16)

    blocks(NE * SEL // 128, 128, select)

    def rest_features(at):
        rft[at, :] = jnp.maximum(dot_nt(wrt[at, :], xs[...]), 0.0).astype(BF16)

    blocks(NE * SEL // 256, 256, rest_features)
    pt[...] = jnp.maximum(dot_nt(pt[...], xs[...]), 0.0).astype(BF16)

    for y in range(4):
        pl.when(lq == y)(lambda: arrived(wt.at[:, y, :, lanes(core * 4, 3)], r_p.at[y]))
        pl.when(lq != y)(lambda: arrived(wt.at[:, y, :, lanes(core * 4, 4)], r_p.at[y]))
        pass_weight(y)
    for y in range(4):
        arrived(wt.at[:, y, :, lanes(4 - core * 4, 4)], r_m.at[y])

    def panel_features(at):
        pf[at, :] = jnp.maximum(dot_nt(xs[at, :], wt[...].reshape(N, DIN)), 0.0).astype(BF16)

    blocks(rows // 256, 256, panel_features)

    mine = dot_nn(pt[...], pf[...])
    for lt in range(8):
        part[lt // 4, lt % 4] = mine[:, lt * 128:lt * 128 + 128].reshape(8, 8, 128)

    def gram_part(k):
        i = (e + k) % NE
        piece = part.at[:, (i // 8 + 4 - zg) % 4, (i % 2) * 4 + (i // 2) % 4]
        return copy(piece, prec.at[k], s_g.at[0], r_g.at[0], e_peer(k))

    unrolled(1, NE, lambda k: gram_part(k).start())

    def rest_gram(c):
        at = pl.ds(pl.multiple_of(c * HALF, HALF), HALF)
        rsend[c] = dot_nn(rft[at, :], pf[...]).reshape(NQ, SEL, N)

    rest_half = copy(rsend.at[1 - core], rmate, s_h.at[0], r_h.at[0], mate)
    rest_gram(1 - core)
    rest_half.start()
    arrived(prec.at[pl.ds(1, NE - 1)], r_g.at[0])
    total = part[:, (lq + 4 - zg) % 4, rg]
    for k in range(1, NE):
        total = total + prec[k]
    zb[:, z] = total
    unrolled(1, NZ, lambda k: copy(zb.at[:, z], zb.at[:, z], s_z.at[0], r_z.at[0], z_peer(k)).start())
    rest_gram(core)
    arrived(zb.at[:, pl.ds(0, NZ - 1)], r_z.at[0])

    parts = (pl.ds(0, 1), pl.ds(1, 3), pl.ds(4, 2))
    for p in range(4):
        gb[core, chip, p] = zb[0, pl.ds(((lq + 4 - p) % 4) * 4, 4)]
    gb[core, chip, 4:] = zb[1, 8:].reshape(2, 4, 8, 128)

    def send_panels(i):
        piece = gb.at[core, chip, parts[i]]
        unrolled(1, NQ, lambda k: copy(piece, piece, s_a.at[i], r_a.at[i], chip_peer(k)).start())

    def pass_panels(i):
        arrived(gb.at[core, pl.ds(0, NQ - 1), parts[i]], r_a.at[i])
        piece = gb.at[core, :, parts[i]]
        copy(piece, piece, s_b.at[i], r_b.at[i], mate).start()

    def wait_panels(i):
        arrived(gb.at[1 - core, :, parts[i]], r_b.at[i])

    def panel(c):
        tiles = []
        for zz in range(2 * c, NZ):
            q = (c + zz // 4) % 4
            slot = c if c < 4 else 4 + zz // 4 - 2
            tiles += [gb[i // 4, q * 4 + i % 4, slot, zz % 4] for i in range(8)]
        return jnp.concatenate(tiles, axis=0)

    send_panels(0)
    send_panels(1)
    send_panels(2)

    rest_half.wait_recv()

    def add_mate(i):
        rsend[core, i] = rsend[core, i] + rmate[i]

    each(0, NQ, add_mate)
    unrolled(1, NQ, lambda k: copy(rsend.at[core, (chip + k) % NQ], rrecv.at[k], s_r.at[0], r_r.at[0], chip_peer(k)).start())

    ri = lax.broadcasted_iota(jnp.int32, (B, B), 0)
    ci = lax.broadcasted_iota(jnp.int32, (B, B), 1)
    eye = (ri == ci).astype(F32)

    def step(j):
        for c in range(N // B):
            @pl.when(j == c)
            def _():
                r0 = c * B
                if c == 0:
                    pass_panels(0)
                if c in (0, 1, 4):
                    wait_panels((0, 1, 4).index(c))
                a = panel(c) * scale
                a = jnp.concatenate([a[:B] + eye] + ([a[B:]] if r0 + B < N else []), axis=0)
                if c:
                    b2 = jnp.concatenate([hi_s[r0:r0 + B, :r0], lo_s[r0:r0 + B, :r0]], axis=0)
                    a = a - times_split(hi_s[r0:, :r0], lo_s[r0:, :r0], b2)
                pan[r0:, :] = a
                w[:, :B] = a[:B, :]
                w[:, B:] = eye

                if c in (0, 2):
                    pass_panels(1 + c // 2)

        factor(w)
        for c in range(N // B):
            @pl.when(j == c)
            def _():
                r0 = c * B
                t2 = jnp.concatenate(split(w[:, B:]), axis=0)
                tts[c] = t2
                ah, al = split(pan[r0:, :])
                lp = times_split(ah, al, t2)
                lp = jnp.concatenate([jnp.where(ri >= ci, lp[:B], 0.0)] + ([lp[B:]] if r0 + B < N else []), axis=0)
                h, l = split(lp)
                hi_s[r0:, r0:r0 + B] = h
                lo_s[r0:, r0:r0 + B] = l
                pan[r0:, :] = lp
                ours = pan[pl.ds(pl.multiple_of(z * own, own), own), :]
                panel_out[:, r0:r0 + B] = jnp.where(z >= 2 * c, ours, 0.0)

    each(0, N // B, step)

    arrived(rrecv.at[pl.ds(1, NQ - 1)], r_r.at[0])
    total = lax.fori_loop(1, NQ, lambda k, t: t + rrecv[k], rsend[core, chip]) * scale
    for c in range(N // B):
        r0 = c * B
        a = total[:, r0:r0 + B]
        if c:
            b2 = jnp.concatenate([hi_s[r0:r0 + B, :r0], lo_s[r0:r0 + B, :r0]], axis=0)
            a = a - times_split(xh[:SEL, :r0], xl[:SEL, :r0], b2)
        ah, al = split(a)
        a = times_split(ah, al, tts[c])
        rest_out[:, r0:r0 + B] = a[:share]
        h, l = split(a)
        xh[:SEL, r0:r0 + B] = h
        xl[:SEL, r0:r0 + B] = l

    arrived(wt.at[pl.ds(0, NZ - 1), lq, :, lanes(rg)], s_w.at[0])
    arrived(wt.at[:, 0:3, :, lanes(0, 5)], s_p.at[0])
    for y in range(4):
        arrived(wt.at[:, y, :, lanes(core * 4, 4)], s_m.at[y])
    arrived(prec.at[pl.ds(1, NE - 1)], s_g.at[0])
    arrived(zb.at[:, pl.ds(0, NZ - 1)], s_z.at[0])
    rest_half.wait_send()
    arrived(rrecv.at[pl.ds(1, NQ - 1)], s_r.at[0])
    for i in range(3):
        arrived(gb.at[core, pl.ds(0, NQ - 1), parts[i]], s_a.at[i])
        arrived(gb.at[core, :, parts[i]], s_b.at[i])


def on_device(samples, counts, panel_weight, rest_weight):
    rows = samples.shape[0]
    own, wide = panel_weight.shape[1], rest_weight.shape[1]
    share = wide // NE
    vmem, anywhere = pl.BlockSpec(memory_space=pltpu.VMEM), pl.BlockSpec(memory_space=pltpu.HBM)
    counted = [1, 1, 1, 4, 4, 4, 1, 1, 1, 1, 3, 3, 3, 3, 1, 1, 1, 1]
    return pl.pallas_call(
        functools.partial(kernel, share, 1.0 / (rows * NE)),
        out_shape=(jax.ShapeDtypeStruct((own, N), F32), jax.ShapeDtypeStruct((share, N), F32)),
        in_specs=[anywhere, pl.BlockSpec(memory_space=pltpu.SMEM), anywhere, anywhere],
        out_specs=(vmem, vmem),
        scratch_shapes=[
            pltpu.VMEM((rows, DIN), BF16),
            pltpu.VMEM((wide, DIN), BF16),
            pltpu.VMEM((NZ, 4, 16, DIN), BF16),
            pltpu.VMEM((rows, N), BF16),
            pltpu.VMEM((NE * SEL, DIN), BF16),
            pltpu.VMEM((NE * SEL, rows), BF16),
            pltpu.VMEM((own, rows), BF16),
            pltpu.VMEM((2, 4, 8, 8, 128), F32),
            pltpu.VMEM((NE, 2, 8, 128), F32),
            pltpu.VMEM((2, NZ, 8, 128), F32),
            pltpu.VMEM((2, NQ, 6, 4, 8, 128), F32),
            pltpu.VMEM((2, NQ, SEL, N), F32),
            pltpu.VMEM((NQ, SEL, N), F32),
            pltpu.VMEM((NQ, SEL, N), F32),
            pltpu.VMEM((B, 2 * B), F32),
            pltpu.VMEM((N, B), F32),
            pltpu.VMEM((N, N), BF16),
            pltpu.VMEM((N, N), BF16),
            pltpu.VMEM((8, 2 * B, B), BF16),
            pltpu.VMEM((32, N), BF16),
            pltpu.VMEM((32, N), BF16),
            pltpu.SemaphoreType.DMA((4,)),
            [pltpu.SemaphoreType.DMA((c,)) for c in counted],
        ],
        compiler_params=pltpu.CompilerParams(
            collective_id=0, has_side_effects=True, vmem_limit_bytes=60 * 2**20
        ),
        cost_estimate=pl.CostEstimate(flops=10 * 2**30, bytes_accessed=8 * 2**20, transcendentals=0),
    )(samples, counts, panel_weight.T, rest_weight.T)


def solution(mesh):
    in_specs = (P("ex", None), P("ex"), P(None, "fac"), P(None, "fac"))
    out_specs = (P("fac", None), P(("fac", "ex"), None))
    return jax.shard_map(
        on_device, mesh=mesh, in_specs=in_specs, out_specs=out_specs, check_vma=False
    )
```

```python
import functools

import jax
import jax.numpy as jnp
from jax import lax
from jax.experimental import pallas as pl
from jax.experimental.pallas import tpu as pltpu
from jax.sharding import PartitionSpec as P

F32, BF16 = jnp.float32, jnp.bfloat16
MESH = pl.DeviceIdType.MESH
N, DIN, B, MB = 1024, 1024, 128, 16
NE, NZ, NQ = 32, 16, 16
SEL = 24
HALF = NQ * SEL
FIRST = (0, 1, 2, 4)
REST_FROM = 7


def split(x):
    hi = x.astype(BF16)
    return hi, (x - hi.astype(F32)).astype(BF16)


def dot_nt(a, b):
    return lax.dot_general(a, b, (((1,), (1,)), ((), ())), preferred_element_type=F32)


def dot_nn(a, b):
    return jnp.dot(a, b, preferred_element_type=F32)


def dot_tn(a, b):
    return lax.dot_general(a, b, (((0,), (0,)), ((), ())), preferred_element_type=F32)


def times_split(hi, lo, b2):
    x = dot_nt(hi, b2)
    return x[:, :B] + x[:, B:] + dot_nt(lo, b2[:B])


def factor(w, beside):
    row = lax.broadcasted_iota(jnp.int32, (MB, B), 0)
    parts = B // MB
    R = w[:MB, :]
    for m in range(parts):
        r0 = m * MB
        G = R
        C = jnp.stack([jnp.broadcast_to(R[:, r0 + t:r0 + t + 1], (MB, B)) for t in range(MB)], axis=0)
        last = m == parts - 1
        if not last:
            low = w[r0 + MB:, :]
            ah, al = split(low[:, r0:r0 + MB])
            lhs = jnp.concatenate([ah, al, ah], axis=1)
        S = jnp.ones((MB, B), F32)
        V = jnp.ones((MB, B), F32)
        for j in range(MB):
            c = C[0]
            d = jnp.broadcast_to(c[j:j + 1, :], (MB, B))
            inv = 1.0 / d
            S = jnp.where(row >= j, lax.rsqrt(d), S)
            V = jnp.where(row >= j, inv, V)
            mult = jnp.where(row != j, c * inv, 0.0)
            if j < MB - 1:
                down = jnp.where(row > j, mult, 0.0)
                R = R - jnp.concatenate([down, down], axis=1) * R[j:j + 1, :]
                C = C[1:] - mult[None] * C[1:, j:j + 1, :]
            G = G - jnp.concatenate([mult, mult], axis=1) * G[j:j + 1, :]
        U = R * jnp.concatenate([S, S], axis=1)
        if not last:
            zh, zl = split(G * jnp.concatenate([V, V], axis=1))
            rhs = jnp.concatenate([zh, zh, zl], axis=0)
            rest = low - jnp.dot(lhs, rhs, preferred_element_type=F32)
            R = rest[:MB]
            w[r0 + MB:, :] = rest
        w[r0:r0 + MB, :] = U
        for f in beside[len(beside) * m // parts:len(beside) * (m + 1) // parts]:
            f()


def cholesky(gram, w, tts, hi_s, lo_s, p_hi, p_lo, dn, extra, before):
    ri = lax.broadcasted_iota(jnp.int32, (B, B), 0)
    ci = lax.broadcasted_iota(jnp.int32, (B, B), 1)
    eye = (ri == ci).astype(F32)
    nb = N // B
    def rows_of(c):
        return jnp.concatenate([hi_s[c * B:c * B + B, :c * B], lo_s[c * B:c * B + B, :c * B]], axis=0)

    def store(r0, r1, c, x):
        h, l = split(x)
        hi_s[r0:r1, c * B:c * B + B] = h
        lo_s[r0:r1, c * B:c * B + B] = l

    def solved(r0, r1, c):
        store(r0, r1, c, times_split(p_hi[c % 2, r0:r1, :], p_lo[c % 2, r0:r1, :], tts[c]))

    def updated(r0, r1, c):
        a = gram(c, r0, r1)
        if c:
            a = a - times_split(hi_s[r0:r1, :c * B], lo_s[r0:r1, :c * B], rows_of(c))
        h, l = split(a)
        p_hi[c % 2, r0:r1, :] = h
        p_lo[c % 2, r0:r1, :] = l

    def next_diag(c):
        k = (c - 1) * B
        r0 = c * B
        a = gram(c, r0, r0 + B) + eye
        if k:
            b2 = jnp.concatenate([hi_s[r0:r0 + B, :k], lo_s[r0:r0 + B, :k]], axis=0)
            a = a - times_split(hi_s[r0:r0 + B, :k], lo_s[r0:r0 + B, :k], b2)
        dn[...] = a

    before(0)
    d = gram(0, 0, B) + eye
    for c in range(nb):
        r0 = c * B
        wc = w.at[c % 2]
        wc[:, :B] = d
        wc[:, B:] = eye
        work = extra(c)
        if c + 1 < nb:
            for r in [(r0 + B, r0 + 2 * B)] + [(i, min(i + 2 * B, N)) for i in range(r0 + 2 * B, N, 2 * B)]:
                if c:
                    work.append(functools.partial(solved, *r, c - 1))
                work.append(functools.partial(updated, *r, c))
            work.append(functools.partial(before, c + 1))
            work.append(functools.partial(next_diag, c + 1))
        factor(wc, work)
        t2 = jnp.concatenate(split(wc[:, B:]), axis=0)
        tts[c] = t2
        u = jnp.where(ri <= ci, wc[:, :B], 0.0)
        store(r0, r0 + B, c, u.T)
        if c + 1 < nb:
            x = times_split(p_hi[c % 2, r0 + B:r0 + 2 * B, :], p_lo[c % 2, r0 + B:r0 + 2 * B, :], t2)
            h, l = split(x)
            hi_s[r0 + B:r0 + 2 * B, r0:r0 + B] = h
            lo_s[r0 + B:r0 + 2 * B, r0:r0 + B] = l
            d = dn[...] - times_split(h, l, jnp.concatenate([h, l], axis=0))


def kernel(share, scale, x_ref, n_ref, wp_ref, wr_ref, panel_out, rest_out,
           xs, wr, wt, pf, wrt, rft, pt, part, prec, zb, gb, rsend, rmate, rrecv, rtot, ra,
           w, hi_s, lo_s, p_hi, p_lo, dn, tts, xh, xl, loc, sems):
    e, z = lax.axis_index("ex"), lax.axis_index("fac")
    chip, core = e // 2, e % 2
    mate = {"ex": chip * 2 + 1 - core}
    lq, rg, zg = chip // 4, core * 4 + chip % 4, z // 4
    rows, own, wide = xs.shape[0], wp_ref.shape[0], wr_ref.shape[0]
    (s_w, r_w, s_p, r_p, s_m, r_m, s_g, r_g, s_z, r_z, s_a, r_a, s_b, r_b, s_r, r_r, s_h, r_h) = sems

    def z_peer(k):
        return {"fac": (z + k) % NZ}

    def e_peer(k):
        return {"ex": (e + k) % NE}

    def chip_peer(k):
        return {"ex": ((chip + k) % NQ) * 2 + core}

    def each(lo, hi, body):
        def run(k, _):
            body(k)
            return 0
        lax.fori_loop(lo, hi, run, 0)

    def unrolled(lo, hi, body):
        for k in range(lo, hi):
            body(k)

    def blocks(count, span, body):
        each(0, count, lambda i: body(pl.ds(pl.multiple_of(i * span, span), span)))

    def copy(src, dst, send, recv, device):
        return pltpu.make_async_remote_copy(src, dst, send, recv, device_id=device, device_id_type=MESH)

    def arrived(ref, sem):
        pltpu.make_async_copy(ref, ref, sem).wait()

    def lanes(i, count=1):
        return pl.ds(pl.multiple_of(i * 128, 128), 128 * count)

    barrier = pltpu.get_barrier_semaphore()
    unrolled(1, NZ, lambda k: pl.semaphore_signal(barrier, inc=1, device_id=z_peer(k), device_id_type=MESH))
    unrolled(1, NE, lambda k: pl.semaphore_signal(barrier, inc=1, device_id=e_peer(k), device_id_type=MESH))
    own_tile = wp_ref.at[pl.ds(pl.multiple_of(lq * 16, 16), 16), lanes(rg)]
    local = [
        pltpu.make_async_copy(own_tile, wt.at[z, lq, :, lanes(rg)], loc.at[0]),
        pltpu.make_async_copy(x_ref, xs, loc.at[1]),
        pltpu.make_async_copy(wr_ref, wr, loc.at[2]),
        pltpu.make_async_copy(wp_ref, pt, loc.at[3]),
    ]
    for c in local:
        c.start()
    pl.semaphore_wait(barrier, NZ - 1 + NE - 1)

    def z_weight(k):
        return copy(own_tile, wt.at[z, lq, :, lanes(rg)], s_w.at[0], r_w.at[0], z_peer(k))

    unrolled(1, NZ, lambda k: z_weight(k).start())
    local[0].wait()
    arrived(wt.at[pl.ds(0, NZ - 1), lq, :, lanes(rg)], r_w.at[0])

    tile = wt.at[:, lq, :, lanes(rg)]
    unrolled(1, NQ, lambda k: copy(tile, tile, s_p.at[0], r_p.at[lq], chip_peer(k)).start())

    def pass_weight(y):
        piece = wt.at[:, y, :, lanes(core * 4, 4)]
        copy(piece, piece, s_m.at[y], r_m.at[y], mate).start()

    for c in local[1:]:
        c.wait()

    def mask(at):
        live = lax.broadcasted_iota(jnp.int32, (256, 1), 0) + at.start < n_ref[0]
        xs[at, :] = jnp.where(live, xs[at, :].astype(F32), 0.0).astype(BF16)

    blocks(rows // 256, 256, mask)

    def select(at):
        c = (lax.broadcasted_iota(jnp.int32, (128, 1), 0) + at.start).astype(F32)
        b = jnp.floor((c + 0.5) * (1.0 / SEL))
        t = c - SEL * b
        device = jnp.where(b < NQ, 2 * b, 2 * (b - NQ) + 1)
        want = jnp.where(t < share, device * share + t, -1.0)
        sel = (lax.broadcasted_iota(jnp.int32, (128, wide), 1).astype(F32) == want).astype(BF16)
        wrt[at, :] = dot_nn(sel, wr[...]).astype(BF16)

    blocks(NE * SEL // 128, 128, select)

    def rest_features(at):
        rft[at, :] = jnp.maximum(dot_nt(wrt[at, :], xs[...]), 0.0).astype(BF16)

    blocks(NE * SEL // 256, 256, rest_features)
    pt[...] = jnp.maximum(dot_nt(pt[...], xs[...]), 0.0).astype(BF16)

    for y in range(4):
        pl.when(lq == y)(lambda: arrived(wt.at[:, y, :, lanes(core * 4, 3)], r_p.at[y]))
        pl.when(lq != y)(lambda: arrived(wt.at[:, y, :, lanes(core * 4, 4)], r_p.at[y]))
        pass_weight(y)
    for y in range(4):
        arrived(wt.at[:, y, :, lanes(4 - core * 4, 4)], r_m.at[y])

    def panel_features(at):
        pf[at, :] = jnp.maximum(dot_nt(xs[at, :], wt[...].reshape(N, DIN)), 0.0).astype(BF16)

    blocks(rows // 256, 256, panel_features)

    mine = dot_nn(pt[...], pf[...])
    for lt in range(8):
        part[lt // 4, lt % 4] = mine[:, lt * 128:lt * 128 + 128].reshape(8, 8, 128)

    def gram_part(k):
        i = (e + k) % NE
        piece = part.at[:, (i // 8 + 4 - zg) % 4, (i % 2) * 4 + (i // 2) % 4]
        return copy(piece, prec.at[k], s_g.at[0], r_g.at[0], e_peer(k))

    unrolled(1, NE, lambda k: gram_part(k).start())

    def rest_gram(c):
        at = pl.ds(pl.multiple_of(c * HALF, HALF), HALF)
        rsend[c] = dot_nn(rft[at, :], pf[...]).reshape(NQ, SEL, N)

    rest_half = copy(rsend.at[1 - core], rmate, s_h.at[0], r_h.at[0], mate)
    rest_gram(1 - core)
    rest_half.start()
    arrived(prec.at[pl.ds(1, NE - 1)], r_g.at[0])
    total = part[:, (lq + 4 - zg) % 4, rg]
    for k in range(1, NE):
        total = total + prec[k]
    zb[:, z] = total
    unrolled(1, NZ, lambda k: copy(zb.at[:, z], zb.at[:, z], s_z.at[0], r_z.at[0], z_peer(k)).start())
    rest_gram(core)
    arrived(zb.at[:, pl.ds(0, NZ - 1)], r_z.at[0])

    parts = (pl.ds(0, 1), pl.ds(1, 1), pl.ds(2, 2), pl.ds(4, 2))
    for p in range(4):
        gb[core, chip, p] = zb[0, pl.ds(((lq + 4 - p) % 4) * 4, 4)]
    gb[core, chip, 4:] = zb[1, 8:].reshape(2, 4, 8, 128)

    def send_panels(i):
        piece = gb.at[core, chip, parts[i]]
        unrolled(1, NQ, lambda k: copy(piece, piece, s_a.at[i], r_a.at[i], chip_peer(k)).start())

    def pass_panels(i):
        arrived(gb.at[core, pl.ds(0, NQ - 1), parts[i]], r_a.at[i])
        piece = gb.at[core, :, parts[i]]
        copy(piece, piece, s_b.at[i], r_b.at[i], mate).start()

    def wait_panels(i):
        arrived(gb.at[1 - core, :, parts[i]], r_b.at[i])

    def panel(c, r0, r1):
        tiles = []
        for zz in range(r0 // 64, r1 // 64):
            q = (c + zz // 4) % 4
            slot = c if c < 4 else 4 + zz // 4 - 2
            tiles += [gb[i // 4, q * 4 + i % 4, slot, zz % 4] for i in range(8)]
        return jnp.concatenate(tiles, axis=0)

    for i in range(4):
        send_panels(i)

    rest_half.wait_recv()

    def add_mate(i):
        rsend[core, i] = rsend[core, i] + rmate[i]

    each(0, NQ, add_mate)
    unrolled(1, NQ, lambda k: copy(rsend.at[core, (chip + k) % NQ], rrecv.at[k], s_r.at[0], r_r.at[0], chip_peer(k)).start())

    def rest_ready():
        arrived(rrecv.at[pl.ds(1, NQ - 1)], r_r.at[0])
        rtot[...] = lax.fori_loop(1, NQ, lambda k, t: t + rrecv[k], rsend[core, chip]) * scale

    def rest_update(c):
        r0 = c * B
        a = rtot[:, r0:r0 + B]
        if c:
            b2 = jnp.concatenate([hi_s[r0:r0 + B, :r0], lo_s[r0:r0 + B, :r0]], axis=0)
            a = a - times_split(xh[:SEL, :r0], xl[:SEL, :r0], b2)
        ra[...] = a

    def rest_solve(c):
        r0 = c * B
        a = times_split(*split(ra[...]), tts[c])
        rest_out[:, r0:r0 + B] = a[:share]
        h, l = split(a)
        xh[:SEL, r0:r0 + B] = h
        xl[:SEL, r0:r0 + B] = l

    def beside(c):
        work = []
        if c in (1, 2):
            work.append(lambda: pass_panels(c + 1))
        if c == REST_FROM:
            work.append(rest_ready)
            for k in range(c):
                work += [functools.partial(rest_update, k), functools.partial(rest_solve, k)]
        elif c > REST_FROM:
            work.append(lambda: rest_solve(c - 1))
        if c >= REST_FROM:
            work.append(lambda: rest_update(c))
        return work

    def before(c):
        if c < 2:
            pass_panels(c)
        if c in FIRST:
            wait_panels(FIRST.index(c))

    cholesky(lambda c, r0, r1: panel(c, r0, r1) * scale, w, tts, hi_s, lo_s, p_hi, p_lo, dn, beside, before)
    rest_solve(N // B - 1)
    ours = pl.ds(pl.multiple_of(z * own, own), own)
    below = lax.broadcasted_iota(jnp.int32, (own, N), 1) <= lax.broadcasted_iota(jnp.int32, (own, N), 0) + z * own
    panel_out[...] = jnp.where(below, hi_s[ours, :].astype(F32) + lo_s[ours, :].astype(F32), 0.0)

    arrived(wt.at[pl.ds(0, NZ - 1), lq, :, lanes(rg)], s_w.at[0])
    arrived(wt.at[:, 0:3, :, lanes(0, 5)], s_p.at[0])
    for y in range(4):
        arrived(wt.at[:, y, :, lanes(core * 4, 4)], s_m.at[y])
    arrived(prec.at[pl.ds(1, NE - 1)], s_g.at[0])
    arrived(zb.at[:, pl.ds(0, NZ - 1)], s_z.at[0])
    rest_half.wait_send()
    arrived(rrecv.at[pl.ds(1, NQ - 1)], s_r.at[0])
    for i in range(4):
        arrived(gb.at[core, pl.ds(0, NQ - 1), parts[i]], s_a.at[i])
        arrived(gb.at[core, :, parts[i]], s_b.at[i])


def on_device(samples, counts, panel_weight, rest_weight):
    rows = samples.shape[0]
    own, wide = panel_weight.shape[1], rest_weight.shape[1]
    share = wide // NE
    vmem, anywhere = pl.BlockSpec(memory_space=pltpu.VMEM), pl.BlockSpec(memory_space=pltpu.HBM)
    counted = [1, 1, 1, 4, 4, 4, 1, 1, 1, 1, 4, 4, 4, 4, 1, 1, 1, 1]
    return pl.pallas_call(
        functools.partial(kernel, share, 1.0 / (rows * NE)),
        out_shape=(jax.ShapeDtypeStruct((own, N), F32), jax.ShapeDtypeStruct((share, N), F32)),
        in_specs=[anywhere, pl.BlockSpec(memory_space=pltpu.SMEM), anywhere, anywhere],
        out_specs=(vmem, vmem),
        scratch_shapes=[
            pltpu.VMEM((rows, DIN), BF16),
            pltpu.VMEM((wide, DIN), BF16),
            pltpu.VMEM((NZ, 4, 16, DIN), BF16),
            pltpu.VMEM((rows, N), BF16),
            pltpu.VMEM((NE * SEL, DIN), BF16),
            pltpu.VMEM((NE * SEL, rows), BF16),
            pltpu.VMEM((own, rows), BF16),
            pltpu.VMEM((2, 4, 8, 8, 128), F32),
            pltpu.VMEM((NE, 2, 8, 128), F32),
            pltpu.VMEM((2, NZ, 8, 128), F32),
            pltpu.VMEM((2, NQ, 6, 4, 8, 128), F32),
            pltpu.VMEM((2, NQ, SEL, N), F32),
            pltpu.VMEM((NQ, SEL, N), F32),
            pltpu.VMEM((NQ, SEL, N), F32),
            pltpu.VMEM((SEL, N), F32),
            pltpu.VMEM((SEL, B), F32),
            pltpu.VMEM((2, B, 2 * B), F32),
            pltpu.VMEM((N, N), BF16),
            pltpu.VMEM((N, N), BF16),
            pltpu.VMEM((2, N, B), BF16),
            pltpu.VMEM((2, N, B), BF16),
            pltpu.VMEM((B, B), F32),
            pltpu.VMEM((8, 2 * B, B), BF16),
            pltpu.VMEM((32, N), BF16),
            pltpu.VMEM((32, N), BF16),
            pltpu.SemaphoreType.DMA((4,)),
            [pltpu.SemaphoreType.DMA((c,)) for c in counted],
        ],
        compiler_params=pltpu.CompilerParams(
            collective_id=0, has_side_effects=True, vmem_limit_bytes=60 * 2**20
        ),
        cost_estimate=pl.CostEstimate(flops=10 * 2**30, bytes_accessed=8 * 2**20, transcendentals=0),
    )(samples, counts, panel_weight.T, rest_weight.T)


def solution(mesh):
    in_specs = (P("ex", None), P("ex"), P(None, "fac"), P(None, "fac"))
    out_specs = (P("fac", None), P(("fac", "ex"), None))
    return jax.shard_map(
        on_device, mesh=mesh, in_specs=in_specs, out_specs=out_specs, check_vma=False
    )
```

```python
import functools

import jax
import jax.numpy as jnp
from jax import lax
from jax.experimental import pallas as pl
from jax.experimental.pallas import tpu as pltpu
from jax.sharding import PartitionSpec as P

F32, BF16 = jnp.float32, jnp.bfloat16
MESH = pl.DeviceIdType.MESH
N, DIN, B, MB = 1024, 1024, 128, 16
NE, NZ, NQ = 32, 16, 16
SEL = 24
HALF = NQ * SEL
FIRST = (0, 1, 2, 3, 4)
EARLY = 512
REST_FROM = 7


def split(x):
    hi = x.astype(BF16)
    return hi, (x - hi.astype(F32)).astype(BF16)


def dot_nt(a, b):
    return lax.dot_general(a, b, (((1,), (1,)), ((), ())), preferred_element_type=F32)


def dot_nn(a, b):
    return jnp.dot(a, b, preferred_element_type=F32)


def dot_tn(a, b):
    return lax.dot_general(a, b, (((0,), (0,)), ((), ())), preferred_element_type=F32)


def times_split(hi, lo, b2):
    x = dot_nt(hi, b2)
    return x[:, :B] + x[:, B:] + dot_nt(lo, b2[:B])


def factor(w, beside):
    row = lax.broadcasted_iota(jnp.int32, (MB, B), 0)
    parts = B // MB
    R = w[:MB, :]
    for m in range(parts):
        r0 = m * MB
        G = R
        C = jnp.stack([jnp.broadcast_to(R[:, r0 + t:r0 + t + 1], (MB, B)) for t in range(MB)], axis=0)
        last = m == parts - 1
        if not last:
            low = w[r0 + MB:, :]
            ah, al = split(low[:, r0:r0 + MB])
            lhs = jnp.concatenate([ah, al, ah], axis=1)
        S = jnp.ones((MB, B), F32)
        V = jnp.ones((MB, B), F32)
        for j in range(MB):
            c = C[0]
            d = jnp.broadcast_to(c[j:j + 1, :], (MB, B))
            inv = 1.0 / d
            S = jnp.where(row >= j, lax.rsqrt(d), S)
            V = jnp.where(row >= j, inv, V)
            mult = jnp.where(row != j, c * inv, 0.0)
            if j < MB - 1:
                down = jnp.where(row > j, mult, 0.0)
                R = R - jnp.concatenate([down, down], axis=1) * R[j:j + 1, :]
                C = C[1:] - mult[None] * C[1:, j:j + 1, :]
            G = G - jnp.concatenate([mult, mult], axis=1) * G[j:j + 1, :]
        U = R * jnp.concatenate([S, S], axis=1)
        if not last:
            zh, zl = split(G * jnp.concatenate([V, V], axis=1))
            rhs = jnp.concatenate([zh, zh, zl], axis=0)
            rest = low - jnp.dot(lhs, rhs, preferred_element_type=F32)
            R = rest[:MB]
            w[r0 + MB:, :] = rest
        w[r0:r0 + MB, :] = U
        for f in beside[len(beside) * m // parts:len(beside) * (m + 1) // parts]:
            f()


def cholesky(gram, w, tts, hi_s, lo_s, p_hi, p_lo, dn, extra, before):
    ri = lax.broadcasted_iota(jnp.int32, (B, B), 0)
    ci = lax.broadcasted_iota(jnp.int32, (B, B), 1)
    eye = (ri == ci).astype(F32)
    nb = N // B
    def rows_of(c):
        return jnp.concatenate([hi_s[c * B:c * B + B, :c * B], lo_s[c * B:c * B + B, :c * B]], axis=0)

    def store(r0, r1, c, x):
        h, l = split(x)
        hi_s[r0:r1, c * B:c * B + B] = h
        lo_s[r0:r1, c * B:c * B + B] = l

    def solved(r0, r1, c):
        store(r0, r1, c, times_split(p_hi[c % 2, r0:r1, :], p_lo[c % 2, r0:r1, :], tts[c]))

    def updated(r0, r1, c):
        a = gram(c, r0, r1)
        if c:
            a = a - times_split(hi_s[r0:r1, :c * B], lo_s[r0:r1, :c * B], rows_of(c))
        h, l = split(a)
        p_hi[c % 2, r0:r1, :] = h
        p_lo[c % 2, r0:r1, :] = l

    def next_diag(c):
        k = (c - 1) * B
        r0 = c * B
        a = gram(c, r0, r0 + B) + eye
        if k:
            b2 = jnp.concatenate([hi_s[r0:r0 + B, :k], lo_s[r0:r0 + B, :k]], axis=0)
            a = a - times_split(hi_s[r0:r0 + B, :k], lo_s[r0:r0 + B, :k], b2)
        dn[...] = a

    before(0)
    d = gram(0, 0, B) + eye
    for c in range(nb):
        r0 = c * B
        wc = w.at[c % 2]
        wc[:, :B] = d
        wc[:, B:] = eye
        work = extra(c)
        if c + 1 < nb:
            for r in [(r0 + B, r0 + 2 * B)] + [(i, min(i + 2 * B, N)) for i in range(r0 + 2 * B, N, 2 * B)]:
                if c:
                    work.append(functools.partial(solved, *r, c - 1))
                work.append(functools.partial(updated, *r, c))
            work.append(functools.partial(before, c + 1))
            work.append(functools.partial(next_diag, c + 1))
        factor(wc, work)
        t2 = jnp.concatenate(split(wc[:, B:]), axis=0)
        tts[c] = t2
        u = jnp.where(ri <= ci, wc[:, :B], 0.0)
        store(r0, r0 + B, c, u.T)
        if c + 1 < nb:
            x = times_split(p_hi[c % 2, r0 + B:r0 + 2 * B, :], p_lo[c % 2, r0 + B:r0 + 2 * B, :], t2)
            h, l = split(x)
            hi_s[r0 + B:r0 + 2 * B, r0:r0 + B] = h
            lo_s[r0 + B:r0 + 2 * B, r0:r0 + B] = l
            d = dn[...] - times_split(h, l, jnp.concatenate([h, l], axis=0))


def kernel(share, scale, x_ref, n_ref, wp_ref, wr_ref, panel_out, rest_out,
           xs, wr, wt, pf, wrt, rft, pt, part, prec, zb, gb, rsend, rmate, rrecv, rtot, ra,
           w, hi_s, lo_s, p_hi, p_lo, dn, tts, xh, xl, loc, sems):
    e, z = lax.axis_index("ex"), lax.axis_index("fac")
    chip, core = e // 2, e % 2
    mate = {"ex": chip * 2 + 1 - core}
    lq, rg, zg = chip // 4, core * 4 + chip % 4, z // 4
    rows, own, wide = xs.shape[0], wp_ref.shape[0], wr_ref.shape[0]
    (s_w, r_w, s_p, r_p, s_m, r_m, s_g, r_g, s_z, r_z, s_a, r_a, s_b, r_b, s_r, r_r, s_h, r_h) = sems

    def z_peer(k):
        return {"fac": (z + k) % NZ}

    def e_peer(k):
        return {"ex": (e + k) % NE}

    def chip_peer(k):
        return {"ex": ((chip + k) % NQ) * 2 + core}

    def each(lo, hi, body):
        def run(k, _):
            body(k)
            return 0
        lax.fori_loop(lo, hi, run, 0)

    def unrolled(lo, hi, body):
        for k in range(lo, hi):
            body(k)

    def blocks(count, span, body):
        each(0, count, lambda i: body(pl.ds(pl.multiple_of(i * span, span), span)))

    def copy(src, dst, send, recv, device):
        return pltpu.make_async_remote_copy(src, dst, send, recv, device_id=device, device_id_type=MESH)

    def arrived(ref, sem):
        pltpu.make_async_copy(ref, ref, sem).wait()

    def lanes(i, count=1):
        return pl.ds(pl.multiple_of(i * 128, 128), 128 * count)

    barrier = pltpu.get_barrier_semaphore()
    unrolled(1, NZ, lambda k: pl.semaphore_signal(barrier, inc=1, device_id=z_peer(k), device_id_type=MESH))
    unrolled(1, NE, lambda k: pl.semaphore_signal(barrier, inc=1, device_id=e_peer(k), device_id_type=MESH))
    own_tile = wp_ref.at[pl.ds(pl.multiple_of(lq * 16, 16), 16), lanes(rg)]
    local = [
        pltpu.make_async_copy(own_tile, wt.at[z, lq, :, lanes(rg)], loc.at[0]),
        pltpu.make_async_copy(x_ref, xs, loc.at[1]),
        pltpu.make_async_copy(wr_ref, wr, loc.at[2]),
        pltpu.make_async_copy(wp_ref, pt, loc.at[3]),
    ]
    for c in local:
        c.start()
    pl.semaphore_wait(barrier, NZ - 1 + NE - 1)

    def z_weight(k):
        return copy(own_tile, wt.at[z, lq, :, lanes(rg)], s_w.at[0], r_w.at[0], z_peer(k))

    unrolled(1, NZ, lambda k: z_weight(k).start())
    local[0].wait()
    arrived(wt.at[pl.ds(0, NZ - 1), lq, :, lanes(rg)], r_w.at[0])

    tile = wt.at[:, lq, :, lanes(rg)]
    unrolled(1, NQ, lambda k: copy(tile, tile, s_p.at[0], r_p.at[lq], chip_peer(k)).start())

    def pass_weight(y):
        piece = wt.at[:, y, :, lanes(core * 4, 4)]
        copy(piece, piece, s_m.at[y], r_m.at[y], mate).start()

    for c in local[1:]:
        c.wait()

    def mask(at):
        live = lax.broadcasted_iota(jnp.int32, (256, 1), 0) + at.start < n_ref[0]
        xs[at, :] = jnp.where(live, xs[at, :].astype(F32), 0.0).astype(BF16)

    blocks(rows // 256, 256, mask)

    def select(at):
        c = (lax.broadcasted_iota(jnp.int32, (128, 1), 0) + at.start).astype(F32)
        b = jnp.floor((c + 0.5) * (1.0 / SEL))
        t = c - SEL * b
        device = jnp.where(b < NQ, 2 * b, 2 * (b - NQ) + 1)
        want = jnp.where(t < share, device * share + t, -1.0)
        sel = (lax.broadcasted_iota(jnp.int32, (128, wide), 1).astype(F32) == want).astype(BF16)
        wrt[at, :] = dot_nn(sel, wr[...]).astype(BF16)

    blocks(NE * SEL // 128, 128, select)

    def rest_features(at):
        rft[at, :] = jnp.maximum(dot_nt(wrt[at, :], xs[...]), 0.0).astype(BF16)

    blocks(NE * SEL // 256, 256, rest_features)
    pt[...] = jnp.maximum(dot_nt(pt[...], xs[...]), 0.0).astype(BF16)

    for y in range(4):
        pl.when(lq == y)(lambda: arrived(wt.at[:, y, :, lanes(core * 4, 3)], r_p.at[y]))
        pl.when(lq != y)(lambda: arrived(wt.at[:, y, :, lanes(core * 4, 4)], r_p.at[y]))
        pass_weight(y)
    for y in range(4):
        arrived(wt.at[:, y, :, lanes(4 - core * 4, 4)], r_m.at[y])

    def panel_features(at):
        pf[at, :] = jnp.maximum(dot_nt(xs[at, :], wt[...].reshape(N, DIN)), 0.0).astype(BF16)

    blocks(rows // 256, 256, panel_features)

    mine = dot_nn(pt[...], pf[...])
    for lt in range(8):
        part[lt // 4, lt % 4] = mine[:, lt * 128:lt * 128 + 128].reshape(8, 8, 128)

    def gram_part(k):
        i = (e + k) % NE
        piece = part.at[:, (i // 8 + 4 - zg) % 4, (i % 2) * 4 + (i // 2) % 4]
        return copy(piece, prec.at[k], s_g.at[0], r_g.at[0], e_peer(k))

    unrolled(1, NE, lambda k: gram_part(k).start())

    def rest_gram(c):
        at = pl.ds(pl.multiple_of(c * HALF, HALF), HALF)
        rsend[c] = dot_nn(rft[at, :], pf[...]).reshape(NQ, SEL, N)

    rest_half = copy(rsend.at[1 - core], rmate, s_h.at[0], r_h.at[0], mate)
    rest_gram(1 - core)
    rest_half.start()
    rest_gram(core)
    arrived(prec.at[pl.ds(1, NE - 1)], r_g.at[0])
    total = part[:, (lq + 4 - zg) % 4, rg]
    for k in range(1, NE):
        total = total + prec[k]
    zb[:, z] = total
    unrolled(1, NZ, lambda k: copy(zb.at[:, z], zb.at[:, z], s_z.at[0], r_z.at[0], z_peer(k)).start())

    rest_half.wait_recv()

    def add_mate(i):
        rsend[core, i] = rsend[core, i] + rmate[i]

    each(0, NQ, add_mate)
    columns = (pl.ds(0, EARLY), pl.ds(EARLY, N - EARLY))

    def send_rest(h):
        unrolled(1, NQ, lambda k: copy(
            rsend.at[core, (chip + k) % NQ, :, columns[h]], rrecv.at[k, :, columns[h]], s_r.at[h], r_r.at[h], chip_peer(k)
        ).start())

    send_rest(0)
    arrived(zb.at[:, pl.ds(0, NZ - 1)], r_z.at[0])

    parts = (pl.ds(0, 1), pl.ds(1, 1), pl.ds(2, 1), pl.ds(3, 1), pl.ds(4, 2))
    for p in range(4):
        gb[core, chip, p] = zb[0, pl.ds(((lq + 4 - p) % 4) * 4, 4)]
    gb[core, chip, 4:] = zb[1, 8:].reshape(2, 4, 8, 128)

    def send_panels(i):
        piece = gb.at[core, chip, parts[i]]
        unrolled(1, NQ, lambda k: copy(piece, piece, s_a.at[i], r_a.at[i], chip_peer(k)).start())

    def pass_panels(i):
        arrived(gb.at[core, pl.ds(0, NQ - 1), parts[i]], r_a.at[i])
        piece = gb.at[core, :, parts[i]]
        copy(piece, piece, s_b.at[i], r_b.at[i], mate).start()

    def wait_panels(i):
        arrived(gb.at[1 - core, :, parts[i]], r_b.at[i])

    def panel(c, r0, r1):
        tiles = []
        for zz in range(r0 // 64, r1 // 64):
            q = (c + zz // 4) % 4
            slot = c if c < 4 else 4 + zz // 4 - 2
            tiles += [gb[i // 4, q * 4 + i % 4, slot, zz % 4] for i in range(8)]
        return jnp.concatenate(tiles, axis=0)

    for i in range(5):
        send_panels(i)

    send_rest(1)

    def rest_ready():
        for h in range(2):
            arrived(rrecv.at[pl.ds(1, NQ - 1), :, columns[h]], r_r.at[h])
        rtot[...] = lax.fori_loop(1, NQ, lambda k, t: t + rrecv[k], rsend[core, chip]) * scale

    def rest_update(c):
        r0 = c * B
        a = rtot[:, r0:r0 + B]
        if c:
            b2 = jnp.concatenate([hi_s[r0:r0 + B, :r0], lo_s[r0:r0 + B, :r0]], axis=0)
            a = a - times_split(xh[:SEL, :r0], xl[:SEL, :r0], b2)
        ra[...] = a

    def rest_solve(c):
        r0 = c * B
        a = times_split(*split(ra[...]), tts[c])
        rest_out[:, r0:r0 + B] = a[:share]
        h, l = split(a)
        xh[:SEL, r0:r0 + B] = h
        xl[:SEL, r0:r0 + B] = l

    def beside(c):
        work = []
        if c in (1, 2, 3):
            work.append(lambda: pass_panels(c + 1))
        if c == REST_FROM:
            work.append(rest_ready)
            for k in range(c):
                work += [functools.partial(rest_update, k), functools.partial(rest_solve, k)]
        elif c > REST_FROM:
            work.append(lambda: rest_solve(c - 1))
        if c >= REST_FROM:
            work.append(lambda: rest_update(c))
        return work

    def before(c):
        if c < 2:
            pass_panels(c)
        if c in FIRST:
            wait_panels(FIRST.index(c))

    cholesky(lambda c, r0, r1: panel(c, r0, r1) * scale, w, tts, hi_s, lo_s, p_hi, p_lo, dn, beside, before)
    rest_solve(N // B - 1)
    ours = pl.ds(pl.multiple_of(z * own, own), own)
    below = lax.broadcasted_iota(jnp.int32, (own, N), 1) <= lax.broadcasted_iota(jnp.int32, (own, N), 0) + z * own
    panel_out[...] = jnp.where(below, hi_s[ours, :].astype(F32) + lo_s[ours, :].astype(F32), 0.0)

    arrived(wt.at[pl.ds(0, NZ - 1), lq, :, lanes(rg)], s_w.at[0])
    arrived(wt.at[:, 0:3, :, lanes(0, 5)], s_p.at[0])
    for y in range(4):
        arrived(wt.at[:, y, :, lanes(core * 4, 4)], s_m.at[y])
    arrived(prec.at[pl.ds(1, NE - 1)], s_g.at[0])
    arrived(zb.at[:, pl.ds(0, NZ - 1)], s_z.at[0])
    rest_half.wait_send()
    for h in range(2):
        arrived(rrecv.at[pl.ds(1, NQ - 1), :, columns[h]], s_r.at[h])
    for i in range(5):
        arrived(gb.at[core, pl.ds(0, NQ - 1), parts[i]], s_a.at[i])
        arrived(gb.at[core, :, parts[i]], s_b.at[i])


def on_device(samples, counts, panel_weight, rest_weight):
    rows = samples.shape[0]
    own, wide = panel_weight.shape[1], rest_weight.shape[1]
    share = wide // NE
    vmem, anywhere = pl.BlockSpec(memory_space=pltpu.VMEM), pl.BlockSpec(memory_space=pltpu.HBM)
    counted = [1, 1, 1, 4, 4, 4, 1, 1, 1, 1, 5, 5, 5, 5, 2, 2, 1, 1]
    return pl.pallas_call(
        functools.partial(kernel, share, 1.0 / (rows * NE)),
        out_shape=(jax.ShapeDtypeStruct((own, N), F32), jax.ShapeDtypeStruct((share, N), F32)),
        in_specs=[anywhere, pl.BlockSpec(memory_space=pltpu.SMEM), anywhere, anywhere],
        out_specs=(vmem, vmem),
        scratch_shapes=[
            pltpu.VMEM((rows, DIN), BF16),
            pltpu.VMEM((wide, DIN), BF16),
            pltpu.VMEM((NZ, 4, 16, DIN), BF16),
            pltpu.VMEM((rows, N), BF16),
            pltpu.VMEM((NE * SEL, DIN), BF16),
            pltpu.VMEM((NE * SEL, rows), BF16),
            pltpu.VMEM((own, rows), BF16),
            pltpu.VMEM((2, 4, 8, 8, 128), F32),
            pltpu.VMEM((NE, 2, 8, 128), F32),
            pltpu.VMEM((2, NZ, 8, 128), F32),
            pltpu.VMEM((2, NQ, 6, 4, 8, 128), F32),
            pltpu.VMEM((2, NQ, SEL, N), F32),
            pltpu.VMEM((NQ, SEL, N), F32),
            pltpu.VMEM((NQ, SEL, N), F32),
            pltpu.VMEM((SEL, N), F32),
            pltpu.VMEM((SEL, B), F32),
            pltpu.VMEM((2, B, 2 * B), F32),
            pltpu.VMEM((N, N), BF16),
            pltpu.VMEM((N, N), BF16),
            pltpu.VMEM((2, N, B), BF16),
            pltpu.VMEM((2, N, B), BF16),
            pltpu.VMEM((B, B), F32),
            pltpu.VMEM((8, 2 * B, B), BF16),
            pltpu.VMEM((32, N), BF16),
            pltpu.VMEM((32, N), BF16),
            pltpu.SemaphoreType.DMA((4,)),
            [pltpu.SemaphoreType.DMA((c,)) for c in counted],
        ],
        compiler_params=pltpu.CompilerParams(
            collective_id=0, has_side_effects=True, vmem_limit_bytes=60 * 2**20
        ),
        cost_estimate=pl.CostEstimate(flops=10 * 2**30, bytes_accessed=8 * 2**20, transcendentals=0),
    )(samples, counts, panel_weight.T, rest_weight.T)


def solution(mesh):
    in_specs = (P("ex", None), P("ex"), P(None, "fac"), P(None, "fac"))
    out_specs = (P("fac", None), P(("fac", "ex"), None))
    return jax.shard_map(
        on_device, mesh=mesh, in_specs=in_specs, out_specs=out_specs, check_vma=False
    )
```

```python
import functools

import jax
import jax.numpy as jnp
from jax import lax
from jax.experimental import pallas as pl
from jax.experimental.pallas import tpu as pltpu
from jax.sharding import PartitionSpec as P

F32, BF16 = jnp.float32, jnp.bfloat16
MESH = pl.DeviceIdType.MESH
N, DIN, B, MB = 1024, 1024, 128, 16
NE, NZ, NQ = 32, 16, 16
SEL = 24
HALF = NQ * SEL
EARLY = 512
REST_FROM = 7


def split(x):
    hi = x.astype(BF16)
    return hi, (x - hi.astype(F32)).astype(BF16)


def dot_nt(a, b):
    return lax.dot_general(a, b, (((1,), (1,)), ((), ())), preferred_element_type=F32)


def dot_nn(a, b):
    return jnp.dot(a, b, preferred_element_type=F32)


def dot_tn(a, b):
    return lax.dot_general(a, b, (((0,), (0,)), ((), ())), preferred_element_type=F32)


def times_split(hi, lo, b2):
    x = dot_nt(hi, b2)
    return x[:, :B] + x[:, B:] + dot_nt(lo, b2[:B])


def factor(w, beside):
    row = lax.broadcasted_iota(jnp.int32, (MB, B), 0)
    parts = B // MB
    R = w[:MB, :]
    for m in range(parts):
        r0 = m * MB
        G = R
        C = jnp.stack([jnp.broadcast_to(R[:, r0 + t:r0 + t + 1], (MB, B)) for t in range(MB)], axis=0)
        last = m == parts - 1
        if not last:
            low = w[r0 + MB:, :]
            ah, al = split(low[:, r0:r0 + MB])
            lhs = jnp.concatenate([ah, al, ah], axis=1)
        S = jnp.ones((MB, B), F32)
        V = jnp.ones((MB, B), F32)
        for j in range(MB):
            c = C[0]
            d = jnp.broadcast_to(c[j:j + 1, :], (MB, B))
            inv = 1.0 / d
            S = jnp.where(row >= j, lax.rsqrt(d), S)
            V = jnp.where(row >= j, inv, V)
            mult = jnp.where(row != j, c * inv, 0.0)
            if j < MB - 1:
                down = jnp.where(row > j, mult, 0.0)
                R = R - jnp.concatenate([down, down], axis=1) * R[j:j + 1, :]
                C = C[1:] - mult[None] * C[1:, j:j + 1, :]
            G = G - jnp.concatenate([mult, mult], axis=1) * G[j:j + 1, :]
        U = R * jnp.concatenate([S, S], axis=1)
        if not last:
            zh, zl = split(G * jnp.concatenate([V, V], axis=1))
            rhs = jnp.concatenate([zh, zh, zl], axis=0)
            rest = low - jnp.dot(lhs, rhs, preferred_element_type=F32)
            R = rest[:MB]
            w[r0 + MB:, :] = rest
        w[r0:r0 + MB, :] = U
        for f in beside[len(beside) * m // parts:len(beside) * (m + 1) // parts]:
            f()


def cholesky(gram, w, tts, hi_s, lo_s, p_hi, p_lo, dn, extra, before):
    ri = lax.broadcasted_iota(jnp.int32, (B, B), 0)
    ci = lax.broadcasted_iota(jnp.int32, (B, B), 1)
    eye = (ri == ci).astype(F32)
    nb = N // B
    def rows_of(c):
        return jnp.concatenate([hi_s[c * B:c * B + B, :c * B], lo_s[c * B:c * B + B, :c * B]], axis=0)

    def store(r0, r1, c, x):
        h, l = split(x)
        hi_s[r0:r1, c * B:c * B + B] = h
        lo_s[r0:r1, c * B:c * B + B] = l

    def solved(r0, r1, c):
        store(r0, r1, c, times_split(p_hi[c % 2, r0:r1, :], p_lo[c % 2, r0:r1, :], tts[c]))

    def updated(r0, r1, c):
        a = gram(c, r0, r1)
        if c:
            a = a - times_split(hi_s[r0:r1, :c * B], lo_s[r0:r1, :c * B], rows_of(c))
        h, l = split(a)
        p_hi[c % 2, r0:r1, :] = h
        p_lo[c % 2, r0:r1, :] = l

    def next_diag(c):
        k = (c - 1) * B
        r0 = c * B
        a = gram(c, r0, r0 + B) + eye
        if k:
            b2 = jnp.concatenate([hi_s[r0:r0 + B, :k], lo_s[r0:r0 + B, :k]], axis=0)
            a = a - times_split(hi_s[r0:r0 + B, :k], lo_s[r0:r0 + B, :k], b2)
        dn[...] = a

    before(0)
    d = gram(0, 0, B) + eye
    for c in range(nb):
        r0 = c * B
        wc = w.at[c % 2]
        wc[:, :B] = d
        wc[:, B:] = eye
        work = extra(c)
        if c + 1 < nb:
            for r in [(r0 + B, r0 + 2 * B)] + [(i, min(i + 2 * B, N)) for i in range(r0 + 2 * B, N, 2 * B)]:
                if c:
                    work.append(functools.partial(solved, *r, c - 1))
                work.append(functools.partial(updated, *r, c))
            work.append(functools.partial(before, c + 1))
            work.append(functools.partial(next_diag, c + 1))
        factor(wc, work)
        t2 = jnp.concatenate(split(wc[:, B:]), axis=0)
        tts[c] = t2
        u = jnp.where(ri <= ci, wc[:, :B], 0.0)
        store(r0, r0 + B, c, u.T)
        if c + 1 < nb:
            x = times_split(p_hi[c % 2, r0 + B:r0 + 2 * B, :], p_lo[c % 2, r0 + B:r0 + 2 * B, :], t2)
            h, l = split(x)
            hi_s[r0 + B:r0 + 2 * B, r0:r0 + B] = h
            lo_s[r0 + B:r0 + 2 * B, r0:r0 + B] = l
            d = dn[...] - times_split(h, l, jnp.concatenate([h, l], axis=0))


def kernel(share, scale, x_ref, n_ref, wp_ref, wr_ref, panel_out, rest_out,
           xs, wr, wt, pf, wrt, rft, pt, part, prec, zb, gb, rsend, rmate, rrecv, rtot, ra,
           w, hi_s, lo_s, p_hi, p_lo, dn, tts, xh, xl, loc, sems):
    e, z = lax.axis_index("ex"), lax.axis_index("fac")
    chip, core = e // 2, e % 2
    mate = {"ex": chip * 2 + 1 - core}
    lq, rg, zg = chip // 4, core * 4 + chip % 4, z // 4
    rows, own, wide = xs.shape[0], wp_ref.shape[0], wr_ref.shape[0]
    (s_w, r_w, s_p, r_p, s_m, r_m, s_g, r_g, s_z, r_z, s_a, r_a, s_b, r_b, s_r, r_r, s_h, r_h) = sems

    def z_peer(k):
        return {"fac": (z + k) % NZ}

    def e_peer(k):
        return {"ex": (e + k) % NE}

    def chip_peer(k):
        return {"ex": ((chip + k) % NQ) * 2 + core}

    def each(lo, hi, body):
        def run(k, _):
            body(k)
            return 0
        lax.fori_loop(lo, hi, run, 0)

    def unrolled(lo, hi, body):
        for k in range(lo, hi):
            body(k)

    def blocks(count, span, body):
        each(0, count, lambda i: body(pl.ds(pl.multiple_of(i * span, span), span)))

    def copy(src, dst, send, recv, device):
        return pltpu.make_async_remote_copy(src, dst, send, recv, device_id=device, device_id_type=MESH)

    def arrived(ref, sem):
        pltpu.make_async_copy(ref, ref, sem).wait()

    def lanes(i, count=1):
        return pl.ds(pl.multiple_of(i * 128, 128), 128 * count)

    barrier = pltpu.get_barrier_semaphore()
    unrolled(1, NZ, lambda k: pl.semaphore_signal(barrier, inc=1, device_id=z_peer(k), device_id_type=MESH))
    unrolled(1, NE, lambda k: pl.semaphore_signal(barrier, inc=1, device_id=e_peer(k), device_id_type=MESH))
    own_tile = wp_ref.at[pl.ds(pl.multiple_of(lq * 16, 16), 16), lanes(rg)]
    local = [
        pltpu.make_async_copy(own_tile, wt.at[z, lq, :, lanes(rg)], loc.at[0]),
        pltpu.make_async_copy(x_ref, xs, loc.at[1]),
        pltpu.make_async_copy(wr_ref, wr, loc.at[2]),
        pltpu.make_async_copy(wp_ref, pt, loc.at[3]),
    ]
    local[0].start()
    pl.semaphore_wait(barrier, NZ - 1 + NE - 1)

    def z_weight(k):
        return copy(own_tile, wt.at[z, lq, :, lanes(rg)], s_w.at[0], r_w.at[0], z_peer(k))

    unrolled(1, NZ, lambda k: z_weight(k).start())
    for c in local[1:]:
        c.start()
    local[0].wait()
    arrived(wt.at[pl.ds(0, NZ - 1), lq, :, lanes(rg)], r_w.at[0])

    tile = wt.at[:, lq, :, lanes(rg)]
    unrolled(1, NQ, lambda k: copy(tile, tile, s_p.at[0], r_p.at[lq], chip_peer(k)).start())

    def pass_weight(y):
        piece = wt.at[:, y, :, lanes(core * 4, 4)]
        copy(piece, piece, s_m.at[y], r_m.at[y], mate).start()

    for c in local[1:]:
        c.wait()

    def mask(at):
        live = lax.broadcasted_iota(jnp.int32, (256, 1), 0) + at.start < n_ref[0]
        xs[at, :] = jnp.where(live, xs[at, :].astype(F32), 0.0).astype(BF16)

    blocks(rows // 256, 256, mask)

    def select(at):
        c = (lax.broadcasted_iota(jnp.int32, (128, 1), 0) + at.start).astype(F32)
        b = jnp.floor((c + 0.5) * (1.0 / SEL))
        t = c - SEL * b
        device = jnp.where(b < NQ, 2 * b, 2 * (b - NQ) + 1)
        want = jnp.where(t < share, device * share + t, -1.0)
        sel = (lax.broadcasted_iota(jnp.int32, (128, wide), 1).astype(F32) == want).astype(BF16)
        wrt[at, :] = dot_nn(sel, wr[...]).astype(BF16)

    blocks(NE * SEL // 128, 128, select)

    def rest_features(at):
        rft[at, :] = jnp.maximum(dot_nt(wrt[at, :], xs[...]), 0.0).astype(BF16)

    blocks(NE * SEL // 256, 256, rest_features)
    pt[...] = jnp.maximum(dot_nt(pt[...], xs[...]), 0.0).astype(BF16)

    for y in range(4):
        pl.when(lq == y)(lambda: arrived(wt.at[:, y, :, lanes(core * 4, 3)], r_p.at[y]))
        pl.when(lq != y)(lambda: arrived(wt.at[:, y, :, lanes(core * 4, 4)], r_p.at[y]))
        pass_weight(y)
    for y in range(4):
        arrived(wt.at[:, y, :, lanes(4 - core * 4, 4)], r_m.at[y])

    def panel_features(at):
        pf[at, :] = jnp.maximum(dot_nt(xs[at, :], wt[...].reshape(N, DIN)), 0.0).astype(BF16)

    blocks(rows // 256, 256, panel_features)

    mine = dot_nn(pt[...], pf[...])
    for lt in range(8):
        part[lt // 4, lt % 4] = mine[:, lt * 128:lt * 128 + 128].reshape(8, 8, 128)

    def gram_part(k):
        i = (e + k) % NE
        piece = part.at[:, (i // 8 + 4 - zg) % 4, (i % 2) * 4 + (i // 2) % 4]
        return copy(piece, prec.at[k], s_g.at[0], r_g.at[0], e_peer(k))

    unrolled(1, NE, lambda k: gram_part(k).start())

    def rest_gram(c):
        at = pl.ds(pl.multiple_of(c * HALF, HALF), HALF)
        rsend[c] = dot_nn(rft[at, :], pf[...]).reshape(NQ, SEL, N)

    rest_half = copy(rsend.at[1 - core], rmate, s_h.at[0], r_h.at[0], mate)
    rest_gram(1 - core)
    rest_half.start()
    rest_gram(core)
    arrived(prec.at[pl.ds(1, NE - 1)], r_g.at[0])
    total = part[:, (lq + 4 - zg) % 4, rg]
    for k in range(1, NE):
        total = total + prec[k]
    zb[:, z] = total

    def z_gram(h):
        unrolled(1, NZ, lambda k: copy(zb.at[h, z], zb.at[h, z], s_z.at[h], r_z.at[h], z_peer(k)).start())

    z_gram(0)
    pl.when(z >= 8)(lambda: z_gram(1))

    rest_half.wait_recv()

    def add_mate(i):
        rsend[core, i] = rsend[core, i] + rmate[i]

    each(0, NQ, add_mate)
    columns = (pl.ds(0, EARLY), pl.ds(EARLY, N - EARLY))

    def send_rest(h):
        unrolled(1, NQ, lambda k: copy(
            rsend.at[core, (chip + k) % NQ, :, columns[h]], rrecv.at[k, :, columns[h]], s_r.at[h], r_r.at[h], chip_peer(k)
        ).start())

    send_rest(0)
    arrived(zb.at[0, pl.ds(0, NZ - 1)], r_z.at[0])
    pl.when(z >= 8)(lambda: arrived(zb.at[1, pl.ds(0, 7)], r_z.at[1]))
    pl.when(z < 8)(lambda: arrived(zb.at[1, pl.ds(0, 8)], r_z.at[1]))

    for p in range(4):
        gb[core, chip, p] = zb[0, pl.ds(((lq + 4 - p) % 4) * 4, 4)]
    gb[core, chip, 4:] = zb[1, 8:].reshape(2, 4, 8, 128)

    def rows_of_chips(i):
        return {2: ((0, 2), (3, 4)), 3: ((0, 3),), 4: ((2, 4),)}.get(i, ((0, 4),))

    def has(i, run, otherwise=None):
        if i in (0, 1, 5):
            run()
            return
        yes = {2: lq != 2, 3: lq != 3, 4: lq >= 2}[i]
        pl.when(yes)(run)
        if otherwise is not None:
            pl.when(jnp.logical_not(yes))(otherwise)

    def senders(i):
        return 4 * sum(b - a for a, b in rows_of_chips(i))

    def send_panels(i):
        piece = gb.at[core, chip, i]
        has(i, lambda: unrolled(1, NQ, lambda k: copy(piece, piece, s_a.at[i], r_a.at[i], chip_peer(k)).start()))

    def pass_panels(i):
        n = senders(i)
        has(i, lambda: arrived(gb.at[core, pl.ds(0, n - 1), i], r_a.at[i]), lambda: arrived(gb.at[core, pl.ds(0, n), i], r_a.at[i]))
        for h, (a, b) in enumerate(rows_of_chips(i)):
            piece = gb.at[core, pl.ds(4 * a, 4 * (b - a)), i]
            copy(piece, piece, s_b.at[2 * i + h], r_b.at[2 * i + h], mate).start()

    def wait_panels(i):
        for h, (a, b) in enumerate(rows_of_chips(i)):
            arrived(gb.at[1 - core, pl.ds(4 * a, 4 * (b - a)), i], r_b.at[2 * i + h])

    def panel(c, r0, r1):
        tiles = []
        for zz in range(r0 // 64, r1 // 64):
            q = (c + zz // 4) % 4
            slot = c if c < 4 else 4 + zz // 4 - 2
            tiles += [gb[i // 4, q * 4 + i % 4, slot, zz % 4] for i in range(8)]
        return jnp.concatenate(tiles, axis=0)

    for i in (0, 1, 2, 3, 5, 4):
        send_panels(i)

    send_rest(1)

    def rest_ready():
        for h in range(2):
            arrived(rrecv.at[pl.ds(1, NQ - 1), :, columns[h]], r_r.at[h])
        rtot[...] = lax.fori_loop(1, NQ, lambda k, t: t + rrecv[k], rsend[core, chip]) * scale

    def rest_update(c):
        r0 = c * B
        a = rtot[:, r0:r0 + B]
        if c:
            b2 = jnp.concatenate([hi_s[r0:r0 + B, :r0], lo_s[r0:r0 + B, :r0]], axis=0)
            a = a - times_split(xh[:SEL, :r0], xl[:SEL, :r0], b2)
        ra[...] = a

    def rest_solve(c):
        r0 = c * B
        a = times_split(*split(ra[...]), tts[c])
        rest_out[:, r0:r0 + B] = a[:share]
        h, l = split(a)
        xh[:SEL, r0:r0 + B] = h
        xl[:SEL, r0:r0 + B] = l

    def beside(c):
        work = []
        if c in (1, 2, 3):
            work.append(lambda: pass_panels(c + 1 if c < 3 else 5))
        if c == REST_FROM:
            work.append(rest_ready)
            for k in range(c):
                work += [functools.partial(rest_update, k), functools.partial(rest_solve, k)]
        elif c > REST_FROM:
            work.append(lambda: rest_solve(c - 1))
        if c >= REST_FROM:
            work.append(lambda: rest_update(c))
        return work

    def before(c):
        if c < 2:
            pass_panels(c)
        if c < 4:
            wait_panels(c)
        if c == 4:
            pass_panels(4)
            wait_panels(5)
            wait_panels(4)

    cholesky(lambda c, r0, r1: panel(c, r0, r1) * scale, w, tts, hi_s, lo_s, p_hi, p_lo, dn, beside, before)
    rest_solve(N // B - 1)
    ours = pl.ds(pl.multiple_of(z * own, own), own)
    below = lax.broadcasted_iota(jnp.int32, (own, N), 1) <= lax.broadcasted_iota(jnp.int32, (own, N), 0) + z * own
    panel_out[...] = jnp.where(below, hi_s[ours, :].astype(F32) + lo_s[ours, :].astype(F32), 0.0)

    arrived(wt.at[pl.ds(0, NZ - 1), lq, :, lanes(rg)], s_w.at[0])
    arrived(wt.at[:, 0:3, :, lanes(0, 5)], s_p.at[0])
    for y in range(4):
        arrived(wt.at[:, y, :, lanes(core * 4, 4)], s_m.at[y])
    arrived(prec.at[pl.ds(1, NE - 1)], s_g.at[0])
    arrived(zb.at[0, pl.ds(0, NZ - 1)], s_z.at[0])
    pl.when(z >= 8)(lambda: arrived(zb.at[1, pl.ds(0, NZ - 1)], s_z.at[1]))
    rest_half.wait_send()
    for h in range(2):
        arrived(rrecv.at[pl.ds(1, NQ - 1), :, columns[h]], s_r.at[h])
    def panels_sent(i):
        has(i, lambda: arrived(gb.at[core, pl.ds(0, NQ - 1), i], s_a.at[i]))
        for h, (a, b) in enumerate(rows_of_chips(i)):
            arrived(gb.at[core, pl.ds(4 * a, 4 * (b - a)), i], s_b.at[2 * i + h])

    for i in range(6):
        panels_sent(i)


def on_device(samples, counts, panel_weight, rest_weight):
    rows = samples.shape[0]
    own, wide = panel_weight.shape[1], rest_weight.shape[1]
    share = wide // NE
    vmem, anywhere = pl.BlockSpec(memory_space=pltpu.VMEM), pl.BlockSpec(memory_space=pltpu.HBM)
    counted = [1, 1, 1, 4, 4, 4, 1, 1, 2, 2, 6, 6, 12, 12, 2, 2, 1, 1]
    return pl.pallas_call(
        functools.partial(kernel, share, 1.0 / (rows * NE)),
        out_shape=(jax.ShapeDtypeStruct((own, N), F32), jax.ShapeDtypeStruct((share, N), F32)),
        in_specs=[anywhere, pl.BlockSpec(memory_space=pltpu.SMEM), anywhere, anywhere],
        out_specs=(vmem, vmem),
        scratch_shapes=[
            pltpu.VMEM((rows, DIN), BF16),
            pltpu.VMEM((wide, DIN), BF16),
            pltpu.VMEM((NZ, 4, 16, DIN), BF16),
            pltpu.VMEM((rows, N), BF16),
            pltpu.VMEM((NE * SEL, DIN), BF16),
            pltpu.VMEM((NE * SEL, rows), BF16),
            pltpu.VMEM((own, rows), BF16),
            pltpu.VMEM((2, 4, 8, 8, 128), F32),
            pltpu.VMEM((NE, 2, 8, 128), F32),
            pltpu.VMEM((2, NZ, 8, 128), F32),
            pltpu.VMEM((2, NQ, 6, 4, 8, 128), F32),
            pltpu.VMEM((2, NQ, SEL, N), F32),
            pltpu.VMEM((NQ, SEL, N), F32),
            pltpu.VMEM((NQ, SEL, N), F32),
            pltpu.VMEM((SEL, N), F32),
            pltpu.VMEM((SEL, B), F32),
            pltpu.VMEM((2, B, 2 * B), F32),
            pltpu.VMEM((N, N), BF16),
            pltpu.VMEM((N, N), BF16),
            pltpu.VMEM((2, N, B), BF16),
            pltpu.VMEM((2, N, B), BF16),
            pltpu.VMEM((B, B), F32),
            pltpu.VMEM((8, 2 * B, B), BF16),
            pltpu.VMEM((32, N), BF16),
            pltpu.VMEM((32, N), BF16),
            pltpu.SemaphoreType.DMA((4,)),
            [pltpu.SemaphoreType.DMA((c,)) for c in counted],
        ],
        compiler_params=pltpu.CompilerParams(
            collective_id=0, has_side_effects=True, vmem_limit_bytes=60 * 2**20
        ),
        cost_estimate=pl.CostEstimate(flops=10 * 2**30, bytes_accessed=8 * 2**20, transcendentals=0),
    )(samples, counts, panel_weight.T, rest_weight.T)


def solution(mesh):
    in_specs = (P("ex", None), P("ex"), P(None, "fac"), P(None, "fac"))
    out_specs = (P("fac", None), P(("fac", "ex"), None))
    return jax.shard_map(
        on_device, mesh=mesh, in_specs=in_specs, out_specs=out_specs, check_vma=False
    )
```

```python
import functools

import jax
import jax.numpy as jnp
from jax import lax
from jax.experimental import pallas as pl
from jax.experimental.pallas import tpu as pltpu
from jax.sharding import PartitionSpec as P

F32, BF16 = jnp.float32, jnp.bfloat16
MESH = pl.DeviceIdType.MESH
N, DIN, B, MB = 1024, 1024, 128, 16
NE, NZ, NQ = 32, 16, 16
SEL = 24
HALF = NQ * SEL
EARLY = 512
REST_FROM = 7


def split(x):
    hi = x.astype(BF16)
    return hi, (x - hi.astype(F32)).astype(BF16)


def dot_nt(a, b):
    return lax.dot_general(a, b, (((1,), (1,)), ((), ())), preferred_element_type=F32)


def dot_nn(a, b):
    return jnp.dot(a, b, preferred_element_type=F32)


def dot_tn(a, b):
    return lax.dot_general(a, b, (((0,), (0,)), ((), ())), preferred_element_type=F32)


def times_split(hi, lo, b2):
    x = dot_nt(hi, b2)
    return x[:, :B] + x[:, B:] + dot_nt(lo, b2[:B])


def factor(w, beside):
    row = lax.broadcasted_iota(jnp.int32, (MB, B), 0)
    parts = B // MB
    R = w[:MB, :]
    for m in range(parts):
        r0 = m * MB
        G = R
        C = jnp.stack([jnp.broadcast_to(R[:, r0 + t:r0 + t + 1], (MB, B)) for t in range(MB)], axis=0)
        last = m == parts - 1
        if not last:
            low = w[r0 + MB:, :]
            ah, al = split(low[:, r0:r0 + MB])
            lhs = jnp.concatenate([ah, al, ah], axis=1)
        S = jnp.ones((MB, B), F32)
        V = jnp.ones((MB, B), F32)
        for j in range(MB):
            c = C[0]
            d = jnp.broadcast_to(c[j:j + 1, :], (MB, B))
            inv = 1.0 / d
            S = jnp.where(row >= j, lax.rsqrt(d), S)
            V = jnp.where(row >= j, inv, V)
            mult = jnp.where(row != j, c * inv, 0.0)
            if j < MB - 1:
                down = jnp.where(row > j, mult, 0.0)
                R = R - jnp.concatenate([down, down], axis=1) * R[j:j + 1, :]
                C = C[1:] - mult[None] * C[1:, j:j + 1, :]
            G = G - jnp.concatenate([mult, mult], axis=1) * G[j:j + 1, :]
        U = R * jnp.concatenate([S, S], axis=1)
        if not last:
            zh, zl = split(G * jnp.concatenate([V, V], axis=1))
            rhs = jnp.concatenate([zh, zh, zl], axis=0)
            rest = low - jnp.dot(lhs, rhs, preferred_element_type=F32)
            R = rest[:MB]
            w[r0 + MB:, :] = rest
        w[r0:r0 + MB, :] = U
        for f in beside[len(beside) * m // parts:len(beside) * (m + 1) // parts]:
            f()


def cholesky(gram, w, tts, hi_s, lo_s, p_hi, p_lo, dn, extra, before):
    ri = lax.broadcasted_iota(jnp.int32, (B, B), 0)
    ci = lax.broadcasted_iota(jnp.int32, (B, B), 1)
    eye = (ri == ci).astype(F32)
    nb = N // B
    def rows_of(c):
        return jnp.concatenate([hi_s[c * B:c * B + B, :c * B], lo_s[c * B:c * B + B, :c * B]], axis=0)

    def store(r0, r1, c, x):
        h, l = split(x)
        hi_s[r0:r1, c * B:c * B + B] = h
        lo_s[r0:r1, c * B:c * B + B] = l

    def solved(r0, r1, c):
        store(r0, r1, c, times_split(p_hi[c % 2, r0:r1, :], p_lo[c % 2, r0:r1, :], tts[c]))

    def updated(r0, r1, c):
        a = gram(c, r0, r1)
        if c:
            a = a - times_split(hi_s[r0:r1, :c * B], lo_s[r0:r1, :c * B], rows_of(c))
        h, l = split(a)
        p_hi[c % 2, r0:r1, :] = h
        p_lo[c % 2, r0:r1, :] = l

    def next_diag(c):
        k = (c - 1) * B
        r0 = c * B
        a = gram(c, r0, r0 + B) + eye
        if k:
            b2 = jnp.concatenate([hi_s[r0:r0 + B, :k], lo_s[r0:r0 + B, :k]], axis=0)
            a = a - times_split(hi_s[r0:r0 + B, :k], lo_s[r0:r0 + B, :k], b2)
        dn[...] = a

    before(0)
    d = gram(0, 0, B) + eye
    for c in range(nb):
        r0 = c * B
        wc = w.at[c % 2]
        wc[:, :B] = d
        wc[:, B:] = eye
        work = extra(c)
        if c + 1 < nb:
            for r in [(r0 + B, r0 + 2 * B)] + [(i, min(i + 2 * B, N)) for i in range(r0 + 2 * B, N, 2 * B)]:
                if c:
                    work.append(functools.partial(solved, *r, c - 1))
                work.append(functools.partial(updated, *r, c))
            work.append(functools.partial(before, c + 1))
            work.append(functools.partial(next_diag, c + 1))
        factor(wc, work)
        t2 = jnp.concatenate(split(wc[:, B:]), axis=0)
        tts[c] = t2
        u = jnp.where(ri <= ci, wc[:, :B], 0.0)
        store(r0, r0 + B, c, u.T)
        if c + 1 < nb:
            x = times_split(p_hi[c % 2, r0 + B:r0 + 2 * B, :], p_lo[c % 2, r0 + B:r0 + 2 * B, :], t2)
            h, l = split(x)
            hi_s[r0 + B:r0 + 2 * B, r0:r0 + B] = h
            lo_s[r0 + B:r0 + 2 * B, r0:r0 + B] = l
            d = dn[...] - times_split(h, l, jnp.concatenate([h, l], axis=0))


def kernel(share, scale, x_ref, n_ref, wp_ref, wr_ref, panel_out, rest_out,
           xs, wr, wt, pf, wrt, rft, pt, part, prec, zb, gb, rsend, rmate, rrecv, rtot, ra,
           w, hi_s, lo_s, p_hi, p_lo, dn, tts, xh, xl, loc, sems):
    e, z = lax.axis_index("ex"), lax.axis_index("fac")
    chip, core = e // 2, e % 2
    mate = {"ex": chip * 2 + 1 - core}
    lq, rg, zg = chip // 4, core * 4 + chip % 4, z // 4
    rows, own, wide = xs.shape[0], wp_ref.shape[0], wr_ref.shape[0]
    (s_w, r_w, s_p, r_p, s_m, r_m, s_g, r_g, s_z, r_z, s_a, r_a, s_b, r_b, s_r, r_r, s_h, r_h) = sems

    def z_peer(k):
        return {"fac": (z + k) % NZ}

    def e_peer(k):
        return {"ex": (e + k) % NE}

    def chip_peer(k):
        return {"ex": ((chip + k) % NQ) * 2 + core}

    def each(lo, hi, body):
        def run(k, _):
            body(k)
            return 0
        lax.fori_loop(lo, hi, run, 0)

    def unrolled(lo, hi, body):
        for k in range(lo, hi):
            body(k)

    def blocks(count, span, body):
        each(0, count, lambda i: body(pl.ds(pl.multiple_of(i * span, span), span)))

    def copy(src, dst, send, recv, device):
        return pltpu.make_async_remote_copy(src, dst, send, recv, device_id=device, device_id_type=MESH)

    def arrived(ref, sem):
        pltpu.make_async_copy(ref, ref, sem).wait()

    def lanes(i, count=1):
        return pl.ds(pl.multiple_of(i * 128, 128), 128 * count)

    barrier = pltpu.get_barrier_semaphore()
    unrolled(1, NZ, lambda k: pl.semaphore_signal(barrier, inc=1, device_id=z_peer(k), device_id_type=MESH))
    unrolled(1, NE, lambda k: pl.semaphore_signal(barrier, inc=1, device_id=e_peer(k), device_id_type=MESH))
    own_tile = wp_ref.at[pl.ds(pl.multiple_of(lq * 16, 16), 16), lanes(rg)]
    local = [
        pltpu.make_async_copy(own_tile, wt.at[z, lq, :, lanes(rg)], loc.at[0]),
        pltpu.make_async_copy(x_ref, xs, loc.at[1]),
        pltpu.make_async_copy(wr_ref, wr, loc.at[2]),
        pltpu.make_async_copy(wp_ref, pt, loc.at[3]),
    ]
    local[0].start()
    pl.semaphore_wait(barrier, NZ - 1 + NE - 1)

    def z_weight(k):
        return copy(own_tile, wt.at[z, lq, :, lanes(rg)], s_w.at[0], r_w.at[0], z_peer(k))

    unrolled(1, NZ, lambda k: z_weight(k).start())
    for c in local[1:]:
        c.start()
    local[0].wait()
    arrived(wt.at[pl.ds(0, NZ - 1), lq, :, lanes(rg)], r_w.at[0])

    x = chip % 4

    def along_x(piece, send, recv):
        unrolled(1, 4, lambda k: copy(piece, piece, send, recv, {"ex": (lq * 4 + (x + k) % 4) * 2 + core}).start())

    def along_y(piece, send, recv):
        unrolled(1, 4, lambda k: copy(piece, piece, send, recv, {"ex": (((lq + k) % 4) * 4 + x) * 2 + core}).start())

    def row_tiles(y, first=core * 4, count=4):
        return wt.at[0:8, y, :, lanes(first, count)]

    def column_tiles(i, count=4):
        return wt.at[8:16, pl.ds(0, count), :, lanes(i)]

    along_x(row_tiles(lq, rg, 1), s_p.at[0], r_p.at[0])
    along_y(wt.at[8:16, lq, :, lanes(rg)], s_p.at[1], r_p.at[1])

    for c in local[1:]:
        c.wait()

    def mask(at):
        live = lax.broadcasted_iota(jnp.int32, (256, 1), 0) + at.start < n_ref[0]
        xs[at, :] = jnp.where(live, xs[at, :].astype(F32), 0.0).astype(BF16)

    blocks(rows // 256, 256, mask)
    arrived(row_tiles(lq, core * 4, 3), r_p.at[0])
    along_y(row_tiles(lq), s_p.at[2], r_p.at[2 + lq])
    arrived(column_tiles(rg, 3), r_p.at[1])
    along_x(column_tiles(rg), s_p.at[3], r_p.at[6 + x])

    def select(at):
        c = (lax.broadcasted_iota(jnp.int32, (128, 1), 0) + at.start).astype(F32)
        b = jnp.floor((c + 0.5) * (1.0 / SEL))
        t = c - SEL * b
        device = jnp.where(b < NQ, 2 * b, 2 * (b - NQ) + 1)
        want = jnp.where(t < share, device * share + t, -1.0)
        sel = (lax.broadcasted_iota(jnp.int32, (128, wide), 1).astype(F32) == want).astype(BF16)
        wrt[at, :] = dot_nn(sel, wr[...]).astype(BF16)

    blocks(NE * SEL // 128, 128, select)

    def rest_features(at):
        rft[at, :] = jnp.maximum(dot_nt(wrt[at, :], xs[...]), 0.0).astype(BF16)

    blocks(NE * SEL // 256, 256, rest_features)
    pt[...] = jnp.maximum(dot_nt(pt[...], xs[...]), 0.0).astype(BF16)

    for i in range(4):
        pl.when(lq != i)(lambda: arrived(row_tiles(i), r_p.at[2 + i]))
        copy(row_tiles(i), row_tiles(i), s_m.at[i], r_m.at[i], mate).start()
        there = column_tiles(core * 4 + i)
        pl.when(x != i)(lambda: arrived(there, r_p.at[6 + i]))
        copy(there, there, s_m.at[4 + i], r_m.at[4 + i], mate).start()
    for i in range(4):
        arrived(row_tiles(i, 4 - core * 4), r_m.at[i])
        arrived(column_tiles(4 - core * 4 + i), r_m.at[4 + i])

    def panel_features(at):
        pf[at, :] = jnp.maximum(dot_nt(xs[at, :], wt[...].reshape(N, DIN)), 0.0).astype(BF16)

    blocks(rows // 256, 256, panel_features)

    mine = dot_nn(pt[...], pf[...])
    for lt in range(8):
        part[lt // 4, lt % 4] = mine[:, lt * 128:lt * 128 + 128].reshape(8, 8, 128)

    def gram_part(k):
        i = (e + k) % NE
        piece = part.at[:, (i // 8 + 4 - zg) % 4, (i % 2) * 4 + (i // 2) % 4]
        return copy(piece, prec.at[k], s_g.at[0], r_g.at[0], e_peer(k))

    unrolled(1, NE, lambda k: gram_part(k).start())

    def rest_gram(c):
        at = pl.ds(pl.multiple_of(c * HALF, HALF), HALF)
        rsend[c] = dot_nn(rft[at, :], pf[...]).reshape(NQ, SEL, N)

    rest_half = copy(rsend.at[1 - core], rmate, s_h.at[0], r_h.at[0], mate)
    rest_gram(1 - core)
    rest_half.start()
    rest_gram(core)
    arrived(prec.at[pl.ds(1, NE - 1)], r_g.at[0])
    total = part[:, (lq + 4 - zg) % 4, rg]
    for k in range(1, NE):
        total = total + prec[k]
    zb[:, z] = total

    def z_gram(h):
        unrolled(1, NZ, lambda k: copy(zb.at[h, z], zb.at[h, z], s_z.at[h], r_z.at[h], z_peer(k)).start())

    z_gram(0)
    pl.when(z >= 8)(lambda: z_gram(1))

    rest_half.wait_recv()

    def add_mate(i):
        rsend[core, i] = rsend[core, i] + rmate[i]

    each(0, NQ, add_mate)
    columns = (pl.ds(0, EARLY), pl.ds(EARLY, N - EARLY))

    def send_rest(h):
        unrolled(1, NQ, lambda k: copy(
            rsend.at[core, (chip + k) % NQ, :, columns[h]], rrecv.at[k, :, columns[h]], s_r.at[h], r_r.at[h], chip_peer(k)
        ).start())

    send_rest(0)
    arrived(zb.at[0, pl.ds(0, NZ - 1)], r_z.at[0])
    pl.when(z >= 8)(lambda: arrived(zb.at[1, pl.ds(0, 7)], r_z.at[1]))
    pl.when(z < 8)(lambda: arrived(zb.at[1, pl.ds(0, 8)], r_z.at[1]))

    for p in range(4):
        gb[core, chip, p] = zb[0, pl.ds(((lq + 4 - p) % 4) * 4, 4)]
    gb[core, chip, 4:] = zb[1, 8:].reshape(2, 4, 8, 128)

    def rows_of_chips(i):
        return {2: ((0, 2), (3, 4)), 3: ((0, 3),), 4: ((2, 4),)}.get(i, ((0, 4),))

    def has(i, run, otherwise=None):
        if i in (0, 1, 5):
            run()
            return
        yes = {2: lq != 2, 3: lq != 3, 4: lq >= 2}[i]
        pl.when(yes)(run)
        if otherwise is not None:
            pl.when(jnp.logical_not(yes))(otherwise)

    def senders(i):
        return 4 * sum(b - a for a, b in rows_of_chips(i))

    def send_panels(i):
        piece = gb.at[core, chip, i]
        has(i, lambda: unrolled(1, NQ, lambda k: copy(piece, piece, s_a.at[i], r_a.at[i], chip_peer(k)).start()))

    def pass_panels(i):
        n = senders(i)
        has(i, lambda: arrived(gb.at[core, pl.ds(0, n - 1), i], r_a.at[i]), lambda: arrived(gb.at[core, pl.ds(0, n), i], r_a.at[i]))
        for h, (a, b) in enumerate(rows_of_chips(i)):
            piece = gb.at[core, pl.ds(4 * a, 4 * (b - a)), i]
            copy(piece, piece, s_b.at[2 * i + h], r_b.at[2 * i + h], mate).start()

    def wait_panels(i):
        for h, (a, b) in enumerate(rows_of_chips(i)):
            arrived(gb.at[1 - core, pl.ds(4 * a, 4 * (b - a)), i], r_b.at[2 * i + h])

    def panel(c, r0, r1):
        tiles = []
        for zz in range(r0 // 64, r1 // 64):
            q = (c + zz // 4) % 4
            slot = c if c < 4 else 4 + zz // 4 - 2
            tiles += [gb[i // 4, q * 4 + i % 4, slot, zz % 4] for i in range(8)]
        return jnp.concatenate(tiles, axis=0)

    for i in (0, 1, 2, 3, 5, 4):
        send_panels(i)

    send_rest(1)

    def rest_ready():
        for h in range(2):
            arrived(rrecv.at[pl.ds(1, NQ - 1), :, columns[h]], r_r.at[h])
        rtot[...] = lax.fori_loop(1, NQ, lambda k, t: t + rrecv[k], rsend[core, chip]) * scale

    def rest_update(c):
        r0 = c * B
        a = rtot[:, r0:r0 + B]
        if c:
            b2 = jnp.concatenate([hi_s[r0:r0 + B, :r0], lo_s[r0:r0 + B, :r0]], axis=0)
            a = a - times_split(xh[:SEL, :r0], xl[:SEL, :r0], b2)
        ra[...] = a

    def rest_solve(c):
        r0 = c * B
        a = times_split(*split(ra[...]), tts[c])
        rest_out[:, r0:r0 + B] = a[:share]
        h, l = split(a)
        xh[:SEL, r0:r0 + B] = h
        xl[:SEL, r0:r0 + B] = l

    def beside(c):
        work = []
        if c in (1, 2, 3):
            work.append(lambda: pass_panels(c + 1 if c < 3 else 5))
        if c == REST_FROM:
            work.append(rest_ready)
            for k in range(c):
                work += [functools.partial(rest_update, k), functools.partial(rest_solve, k)]
        elif c > REST_FROM:
            work.append(lambda: rest_solve(c - 1))
        if c >= REST_FROM:
            work.append(lambda: rest_update(c))
        return work

    def before(c):
        if c < 2:
            pass_panels(c)
        if c < 4:
            wait_panels(c)
        if c == 4:
            pass_panels(4)
            wait_panels(5)
            wait_panels(4)

    cholesky(lambda c, r0, r1: panel(c, r0, r1) * scale, w, tts, hi_s, lo_s, p_hi, p_lo, dn, beside, before)
    rest_solve(N // B - 1)
    ours = pl.ds(pl.multiple_of(z * own, own), own)
    below = lax.broadcasted_iota(jnp.int32, (own, N), 1) <= lax.broadcasted_iota(jnp.int32, (own, N), 0) + z * own
    panel_out[...] = jnp.where(below, hi_s[ours, :].astype(F32) + lo_s[ours, :].astype(F32), 0.0)

    arrived(wt.at[pl.ds(0, NZ - 1), lq, :, lanes(rg)], s_w.at[0])
    arrived(row_tiles(0, 0, 3), s_p.at[0])
    arrived(row_tiles(0, 0, 3), s_p.at[1])
    arrived(wt.at[0:8, 0:3, :, lanes(0, 4)], s_p.at[2])
    arrived(wt.at[8:16, 0:3, :, lanes(0, 4)], s_p.at[3])
    for i in range(4):
        arrived(row_tiles(i), s_m.at[i])
        arrived(column_tiles(core * 4 + i), s_m.at[4 + i])
    arrived(prec.at[pl.ds(1, NE - 1)], s_g.at[0])
    arrived(zb.at[0, pl.ds(0, NZ - 1)], s_z.at[0])
    pl.when(z >= 8)(lambda: arrived(zb.at[1, pl.ds(0, NZ - 1)], s_z.at[1]))
    rest_half.wait_send()
    for h in range(2):
        arrived(rrecv.at[pl.ds(1, NQ - 1), :, columns[h]], s_r.at[h])
    def panels_sent(i):
        has(i, lambda: arrived(gb.at[core, pl.ds(0, NQ - 1), i], s_a.at[i]))
        for h, (a, b) in enumerate(rows_of_chips(i)):
            arrived(gb.at[core, pl.ds(4 * a, 4 * (b - a)), i], s_b.at[2 * i + h])

    for i in range(6):
        panels_sent(i)


def on_device(samples, counts, panel_weight, rest_weight):
    rows = samples.shape[0]
    own, wide = panel_weight.shape[1], rest_weight.shape[1]
    share = wide // NE
    vmem, anywhere = pl.BlockSpec(memory_space=pltpu.VMEM), pl.BlockSpec(memory_space=pltpu.HBM)
    counted = [1, 1, 4, 10, 8, 8, 1, 1, 2, 2, 6, 6, 12, 12, 2, 2, 1, 1]
    return pl.pallas_call(
        functools.partial(kernel, share, 1.0 / (rows * NE)),
        out_shape=(jax.ShapeDtypeStruct((own, N), F32), jax.ShapeDtypeStruct((share, N), F32)),
        in_specs=[anywhere, pl.BlockSpec(memory_space=pltpu.SMEM), anywhere, anywhere],
        out_specs=(vmem, vmem),
        scratch_shapes=[
            pltpu.VMEM((rows, DIN), BF16),
            pltpu.VMEM((wide, DIN), BF16),
            pltpu.VMEM((NZ, 4, 16, DIN), BF16),
            pltpu.VMEM((rows, N), BF16),
            pltpu.VMEM((NE * SEL, DIN), BF16),
            pltpu.VMEM((NE * SEL, rows), BF16),
            pltpu.VMEM((own, rows), BF16),
            pltpu.VMEM((2, 4, 8, 8, 128), F32),
            pltpu.VMEM((NE, 2, 8, 128), F32),
            pltpu.VMEM((2, NZ, 8, 128), F32),
            pltpu.VMEM((2, NQ, 6, 4, 8, 128), F32),
            pltpu.VMEM((2, NQ, SEL, N), F32),
            pltpu.VMEM((NQ, SEL, N), F32),
            pltpu.VMEM((NQ, SEL, N), F32),
            pltpu.VMEM((SEL, N), F32),
            pltpu.VMEM((SEL, B), F32),
            pltpu.VMEM((2, B, 2 * B), F32),
            pltpu.VMEM((N, N), BF16),
            pltpu.VMEM((N, N), BF16),
            pltpu.VMEM((2, N, B), BF16),
            pltpu.VMEM((2, N, B), BF16),
            pltpu.VMEM((B, B), F32),
            pltpu.VMEM((8, 2 * B, B), BF16),
            pltpu.VMEM((32, N), BF16),
            pltpu.VMEM((32, N), BF16),
            pltpu.SemaphoreType.DMA((4,)),
            [pltpu.SemaphoreType.DMA((c,)) for c in counted],
        ],
        compiler_params=pltpu.CompilerParams(
            collective_id=0, has_side_effects=True, vmem_limit_bytes=60 * 2**20
        ),
        cost_estimate=pl.CostEstimate(flops=10 * 2**30, bytes_accessed=8 * 2**20, transcendentals=0),
    )(samples, counts, panel_weight.T, rest_weight.T)


def solution(mesh):
    in_specs = (P("ex", None), P("ex"), P(None, "fac"), P(None, "fac"))
    out_specs = (P("fac", None), P(("fac", "ex"), None))
    return jax.shard_map(
        on_device, mesh=mesh, in_specs=in_specs, out_specs=out_specs, check_vma=False
    )
```
